512 devices in a mesh: groups: 8 (over x, core), owners: 64 (over y, z).
Axes of the slice: x: 4, y: 4, z: 16, core: 2. Of those that a mesh axis runs over, the one named last changes fastest.
Arguments:
- vectors: bfloat16 [65536, 768], P(('groups', 'owners')), may hold values from -6 to 6
- list_ids: int32 [65536], P(('groups', 'owners')), may hold values from 0 to 65535, as said below
- codes: int32 [192, 65536], P(None, ('groups', 'owners')), may hold values from 0 to 255
- centroids: bfloat16 [65536, 768], P(('groups', 'owners')), may hold values from -5 to 5
- codebook0: float32 [96, 8, 256], replicated, may hold values from -6 to 6
Outputs:
- codebook: float32 [96, 8, 256], replicated
- list_error: float32 [65536], P(('groups', 'owners'))
The draws below stay inside these ranges and needn't reach their ends.
Inputs may be any that keep to these rules, and one draw needn't show every extreme that they name: `list_ids`: the owner index of list l is (l // 128) % 64. Among the 128 vectors of one device at most 6 lie in lists of one owner index; in each group of 64 consecutive devices one owner index gets exactly 6 vectors from every device of the group.
All inputs are finite; a program needn't handle non-finite values.
Results may differ from the reference program's by a relative error of at most 0.0003.
Values may be sent and summed in bfloat16 or wider, within the bound.
A program may use at most 128 MiB of HBM per device.

```python
import jax
import jax.numpy as jnp
from jax import lax

D = 768
SUBSP = 96
CODES = 256
LIST_DEV = 128
VEC_DEV = 128
SUBDIM = 8
CAP = 6
LISTS = 65536
VECTORS = 65536
PRIOR = 128
N_OWNERS = 64
DEVICES = 512


def draw_list_ids(key, part):
    key = jax.random.fold_in(key, 11)
    group_count = DEVICES // N_OWNERS
    slot_total = N_OWNERS * CAP

    def one_block(block):
        group = block // N_OWNERS
        group_key = jax.random.fold_in(jax.random.fold_in(key, 7), group)
        block_key = jax.random.fold_in(key, block)
        order = jax.random.permutation(group_key, N_OWNERS).astype(jnp.int32)
        rank_of = jnp.zeros((N_OWNERS,), jnp.int32).at[order].set(jnp.arange(N_OWNERS, dtype=jnp.int32))
        slot_ids = jnp.arange(slot_total, dtype=jnp.int32)
        slot_owner = slot_ids // CAP
        slot_pos = slot_ids % CAP
        owner_rank = rank_of[slot_owner]
        limit = jnp.where(owner_rank < N_OWNERS // 4, CAP, CAP // 3)
        priority = jnp.where(owner_rank == 0, 2, jnp.where(slot_pos < limit, 1, 0))
        keys = jax.random.split(block_key, 4)
        noise = jax.random.randint(keys[0], (slot_total,), 0, 4096, dtype=jnp.int32)
        score = (priority * 4096 + noise) * slot_total + slot_ids
        picked = lax.top_k(score, VEC_DEV)[1].astype(jnp.int32)
        owners_picked = picked // CAP
        shuffled = owners_picked[jax.random.permutation(keys[1], VEC_DEV)]
        far_group = jax.random.randint(keys[2], (VEC_DEV,), 0, group_count, dtype=jnp.int32)
        within = jax.random.randint(keys[3], (VEC_DEV,), 0, LIST_DEV, dtype=jnp.int32)
        return far_group * (LIST_DEV * N_OWNERS) + shuffled * LIST_DEV + within
    return jax.vmap(one_block)(jnp.arange(DEVICES, dtype=jnp.int32)).reshape(VECTORS)


def set_ends(array, rng, smallest, high):
    longest = array.shape.index(max(array.shape))
    spots = []
    for shift in (0, 1):
        where = [jax.random.randint(jax.random.fold_in(rng, axis), (), 0, length) for axis, length in enumerate(array.shape)]
        where[longest] = (where[longest] + shift) % array.shape[longest]
        spots.append(tuple(where))
    return array.at[spots[0]].set(smallest).at[spots[1]].set(high)


def shard_levels(key, shape, cuts, least, largest):
    factor_of, own = 1.0, jax.random.fold_in(key, 6)
    for axis_at, blocks in cuts:
        steps = jnp.exp(jax.random.uniform(jax.random.fold_in(own, axis_at), (blocks,), jnp.float32, least / len(cuts), largest / len(cuts)))
        factor_of = factor_of * jnp.repeat(steps, shape[axis_at] // blocks).reshape([-1 if axis == axis_at else 1 for axis in range(len(shape))])
    return factor_of


def normal_values(own_key, dims, spread, most, cuts=(), kind=jnp.bfloat16):
    gain = shard_levels(own_key, dims, cuts, -0.22, 0.18) if cuts else 1.0
    result = jax.random.normal(own_key, dims, jnp.float32) * spread * gain
    return jnp.minimum(jnp.maximum(result, -most), most).astype(kind)


def setup_inputs(seed: int = 0) -> dict:
    key_of = jax.random.split(jax.random.key(seed), 6)
    return {
        "vectors": normal_values(key_of[0], (VECTORS, D), 1.0, 6.0, ((0, 512),)),
        "list_ids": draw_list_ids(jax.random.fold_in(key_of[5], 71), 0),
        "codes": set_ends(jax.random.randint(key_of[2], (2 * SUBSP, VECTORS), 0, CODES), jax.random.fold_in(key_of[2], 1), 0, CODES - 1).astype(jnp.int32),
        "centroids": normal_values(key_of[3], (LISTS, D), 0.7, 5.0, ((0, 512),)),
        "codebook0": normal_values(key_of[4], (SUBSP, SUBDIM, CODES), 1.0, 6.0, (), jnp.float32),
    }


def code_totals_block(residual, codes, sub_count, code_count):
    rows_here, feat_dim = residual.shape
    sub_width = feat_dim // sub_count
    pieces = residual.reshape(rows_here * sub_count, sub_width)
    offsets = (jnp.arange(sub_count, dtype=jnp.int32) * code_count)[None, :]
    weights = jnp.ones((rows_here * sub_count,), jnp.float32)
    sum_list = []
    count_list = []
    for which_refit in range(2):
        targets = (codes[:, which_refit * sub_count:(which_refit + 1) * sub_count] + offsets).reshape(-1)
        sum_list.append(jax.ops.segment_sum(pieces, targets, sub_count * code_count))
        count_list.append(jax.ops.segment_sum(weights, targets, sub_count * code_count))
    return jnp.stack(sum_list), jnp.stack(count_list)


def refit_pair(code_sums, code_counts, start_book, prior_weight):
    first_book = (code_sums[0] + prior_weight * start_book) / (code_counts[0][:, None] + prior_weight)
    return (code_sums[1] + prior_weight * first_book) / (code_counts[1][:, None] + prior_weight)


def vector_errors(residual, codes, book_flat, sub_count, code_count):
    rows_here, feat_dim = residual.shape
    sub_width = feat_dim // sub_count
    offsets = (jnp.arange(sub_count, dtype=jnp.int32) * code_count)[None, :]
    targets = codes[:, sub_count:2 * sub_count] + offsets
    recon = jnp.take(book_flat, targets, axis=0)
    diff = residual.reshape(rows_here, sub_count, sub_width) - recon
    return jnp.sum(diff * diff, axis=(1, 2)) / feat_dim


def block_residual(vectors, list_ids, codes, centroids, index):
    first_row = (index * VEC_DEV).astype(jnp.int32)
    rows = lax.dynamic_slice_in_dim(vectors, first_row, VEC_DEV, 0)
    ids = lax.dynamic_slice_in_dim(list_ids, first_row, VEC_DEV, 0)
    block_codes = lax.dynamic_slice_in_dim(codes, first_row, VEC_DEV, 1).T
    residual = rows.astype(jnp.float32) - jnp.take(centroids, ids, axis=0).astype(jnp.float32)
    return residual, ids, block_codes


def reference(vectors, list_ids, codes, centroids, codebook0):
    block_count = VECTORS // VEC_DEV
    indices = jnp.arange(block_count, dtype=jnp.int32)

    def accumulate(carry, index):
        residual, ids, block_codes = block_residual(vectors, list_ids, codes, centroids, index)
        part_sums, part_counts = code_totals_block(residual, block_codes, SUBSP, CODES)
        return (carry[0] + part_sums, carry[1] + part_counts), None

    start = (jnp.zeros((2, SUBSP * CODES, SUBDIM), jnp.float32), jnp.zeros((2, SUBSP * CODES), jnp.float32))
    (code_sums, code_counts), _ = lax.scan(accumulate, start, indices)
    start_book = jnp.transpose(codebook0, (0, 2, 1)).reshape(SUBSP * CODES, SUBDIM)
    book_flat = refit_pair(code_sums, code_counts, start_book, float(PRIOR))

    def add_errors(carry, index):
        residual, ids, block_codes = block_residual(vectors, list_ids, codes, centroids, index)
        errors = vector_errors(residual, block_codes, book_flat, SUBSP, CODES)
        return carry + jax.ops.segment_sum(errors, ids, LISTS), None

    list_error, _ = lax.scan(add_errors, jnp.zeros((LISTS,), jnp.float32), indices)
    return jnp.transpose(book_flat.reshape(SUBSP, CODES, SUBDIM), (0, 2, 1)), list_error
```

```python
import functools

import jax
import jax.numpy as jnp
from jax import lax
from jax.experimental import pallas as pl
from jax.experimental.pallas import tpu as pltpu
from jax.sharding import PartitionSpec as P

MESH = pl.DeviceIdType.MESH
F32 = jnp.float32
BF16 = jnp.bfloat16
I32 = jnp.int32

ROWS = 128
DIM = 768
SUBS = 96
WIDTH = 8
CODES = 256
OWNERS = 64
GROUPS = 8
CAP = 6
SLOTS = 8
LANES = 128
PAIRS = 3
LISTS_HERE = GROUPS * ROWS
CHUNKS = 32
CHUNK_SUBS = SUBS // CHUNKS
CHUNK_ROWS = 56
PLANE = 16
PRIOR = 128.0
UNIT_PLACES = (0, 2, 5, 8, 10, 13)
VMEM_LIMIT = 48 * 1024 * 1024


def vmem():
    return pl.BlockSpec(memory_space=pltpu.VMEM)


def wait_bytes(ref, sem):
    pltpu.make_async_copy(ref, ref, sem).wait()


def place():
    group, owner = lax.axis_index("groups"), lax.axis_index("owners")
    return group, owner


def fetch_kernel(ids_ref, cent_ref, rows_ref, key_ref, ids_all, table, sendbuf, id_send, id_recv,
                 own_sem, x_send, x_recv, sib_send, sib_recv, row_send, row_recv):
    group, owner = place()
    y, z = owner // 16, owner % 16
    sibling = group + 1 - 2 * (group % 2)

    barrier = pltpu.get_barrier_semaphore()

    def greet(k, _):
        pl.semaphore_signal(barrier, inc=1, device_id=(group, (owner + k) % OWNERS), device_id_type=MESH)
        return 0

    lax.fori_loop(1, OWNERS, greet, 0)
    for k in range(1, GROUPS):
        pl.semaphore_signal(barrier, inc=1, device_id=((group + k) % GROUPS, owner), device_id_type=MESH)
    pl.semaphore_wait(barrier, OWNERS - 1 + GROUPS - 1)

    def id_copy(k):
        return pltpu.make_async_remote_copy(
            ids_ref, ids_all.at[owner], id_send, id_recv, device_id=(group, (owner + k) % OWNERS), device_id_type=MESH)

    own = pltpu.make_async_copy(cent_ref, table.at[group], own_sem)
    own.start()
    across = []
    for j in range(1, 4):
        across.append(pltpu.make_async_remote_copy(
            cent_ref, table.at[group], x_send.at[j - 1], x_recv.at[j - 1],
            device_id=((group + 2 * j) % GROUPS, owner), device_id_type=MESH))
    lax.fori_loop(1, OWNERS, lambda k, _: (id_copy(k).start(), 0)[1], 0)
    for copy in across:
        copy.start()
    aside = [pltpu.make_async_remote_copy(
        cent_ref, table.at[group], sib_send.at[0], sib_recv.at[0], device_id=(sibling, owner), device_id_type=MESH)]
    aside[0].start()
    ids_all[owner] = ids_ref[...]

    wait_bytes(ids_all.at[pl.ds(0, OWNERS - 1)], id_recv)
    ids = ids_all[:, 0, :]
    mine = ((ids >> 7) & (OWNERS - 1)) == owner
    before = (lax.broadcasted_iota(I32, (LANES, LANES), 0) < lax.broadcasted_iota(I32, (LANES, LANES), 1))
    rank = jnp.dot(mine.astype(F32).astype(BF16), before.astype(F32).astype(BF16), preferred_element_type=F32)
    local = (((ids >> 13) << 7) + (ids & 127) + 1).astype(F32)
    key = jnp.where(mine, rank * 2048.0 + local, -1.0)
    key_ref[:, 0, :] = key

    for j in range(1, 4):
        source = (group + 2 * GROUPS - 2 * j) % GROUPS
        across[j - 1].wait_recv()
        relay = pltpu.make_async_remote_copy(
            table.at[source], table.at[source], sib_send.at[j], sib_recv.at[j],
            device_id=(sibling, owner), device_id_type=MESH)
        relay.start()
        aside.append(relay)
    own.wait()
    for copy in aside:
        copy.wait_recv()

    lists = table[...].reshape(LISTS_HERE, DIM)
    list_lane = lax.broadcasted_iota(I32, (16, SLOTS, LISTS_HERE), 2).astype(F32) + 1.0
    slot_base = lax.broadcasted_iota(I32, (16, SLOTS, LANES), 1).astype(F32) * 2048.0

    def row_copy(peer):
        return pltpu.make_async_remote_copy(
            sendbuf.at[peer], rows_ref.at[owner], row_send, row_recv, device_id=(group, peer), device_id_type=MESH)

    def serve(q, _):
        first = ((y + q) % 4) * 16
        at = key_ref[pl.ds(first, 16)] - slot_base
        hit = (at > 0.5) & (at < 1024.5)
        which = jnp.sum(jnp.where(hit, at, 0.0), axis=2, keepdims=True)
        pick = (which == list_lane).astype(F32).reshape(16 * SLOTS, LISTS_HERE).astype(BF16)
        got = jnp.dot(pick, lists, preferred_element_type=F32).reshape(16, SLOTS, DIM)
        for p in range(PAIRS):
            both = jnp.concatenate(
                [got[:, :, 256 * p: 256 * p + 128], got[:, :, 256 * p + 128: 256 * p + 256]], axis=1)
            sendbuf[pl.ds(first, 16), 16 * p: 16 * p + 16, :] = both.astype(BF16)

        def send(k, _):
            peer = first + (z + k) % 16

            @pl.when(peer != owner)
            def _():
                row_copy(peer).start()
            return 0

        lax.fori_loop(0, 16, send, 0)
        return 0

    lax.fori_loop(0, 4, serve, 0)
    rows_ref[owner] = sendbuf[owner]

    for copy in across + aside:
        copy.wait_send()
    wait_bytes(ids_all.at[pl.ds(0, OWNERS - 1)], id_send)
    wait_bytes(sendbuf.at[pl.ds(0, OWNERS - 1)], row_send)
    wait_bytes(sendbuf.at[pl.ds(0, OWNERS - 1)], row_recv)


def fetch_rows(ids_row, centroids):
    return pl.pallas_call(
        fetch_kernel,
        out_shape=(jax.ShapeDtypeStruct((OWNERS, 16 * PAIRS, LANES), BF16),
                   jax.ShapeDtypeStruct((OWNERS, 1, LANES), F32)),
        in_specs=[vmem()] * 2,
        out_specs=(vmem(), vmem()),
        scratch_shapes=[
            pltpu.VMEM((OWNERS, 1, LANES), I32),
            pltpu.VMEM((GROUPS, ROWS, DIM), BF16),
            pltpu.VMEM((OWNERS, 16 * PAIRS, LANES), BF16),
            pltpu.SemaphoreType.DMA, pltpu.SemaphoreType.DMA, pltpu.SemaphoreType.DMA,
            pltpu.SemaphoreType.DMA((3,)), pltpu.SemaphoreType.DMA((3,)),
            pltpu.SemaphoreType.DMA((4,)), pltpu.SemaphoreType.DMA((4,)),
            pltpu.SemaphoreType.DMA, pltpu.SemaphoreType.DMA,
        ],
        compiler_params=pltpu.CompilerParams(collective_id=0, has_side_effects=True, vmem_limit_bytes=VMEM_LIMIT),
    )(ids_row, centroids)


def totals_kernel(ids_ref, rows_ref, vec_ref, codes_ref, sums_ref, resid_ref, stacked):
    ids = ids_ref[...]
    owner = (ids >> 7) & (OWNERS - 1)
    in_owner = (lax.broadcasted_iota(I32, (OWNERS, LANES), 0) == owner).astype(F32)
    before = (lax.broadcasted_iota(I32, (LANES, LANES), 0) < lax.broadcasted_iota(I32, (LANES, LANES), 1))
    running = jnp.dot(in_owner.astype(BF16), before.astype(F32).astype(BF16), preferred_element_type=F32)
    rank = jnp.sum(in_owner * running, axis=0, keepdims=True).astype(I32)
    slot = owner * SLOTS + rank
    place_t = (lax.broadcasted_iota(I32, (OWNERS * SLOTS, LANES), 0) == slot).astype(F32)
    pick = place_t.T.astype(BF16)
    for p in range(PAIRS):
        both = rows_ref[:, 16 * p: 16 * p + 16, :].astype(F32)
        for h in range(2):
            j = 2 * p + h
            block = both[:, 8 * h: 8 * h + 8, :].reshape(OWNERS * SLOTS, LANES).astype(BF16)
            cent_t = jnp.dot(pick, block, preferred_element_type=F32).T
            vec_t = vec_ref[:, 128 * j: 128 * j + 128].astype(F32).T
            resid_ref[128 * j: 128 * j + 128, :] = vec_t - cent_t
            stacked[16 * j: 16 * j + 16] = jnp.concatenate(
                [vec_t.reshape(16, WIDTH, LANES), cent_t.reshape(16, WIDTH, LANES)], axis=1).astype(BF16)

    level = lax.broadcasted_iota(I32, (CODES, LANES), 0)
    ones = jnp.ones((16, LANES), BF16)
    row8 = lax.broadcasted_iota(I32, (8, CODES), 0)

    def chunk(ch, _):
        count_tile = jnp.zeros((8, CODES), F32)
        for mm in range(CHUNK_SUBS):
            m = ch * CHUNK_SUBS + mm
            left = jnp.concatenate([stacked[m], ones], axis=0)
            for r in range(2):
                code = codes_ref[pl.ds(r * SUBS + m, 1), :]
                onehot = (level == code).astype(F32).astype(BF16)
                out = lax.dot_general(left, onehot, (((1,), (1,)), ((), ())), preferred_element_type=F32)
                sums_ref[ch, 16 * mm + 8 * r: 16 * mm + 8 * r + 8, :] = out[0:8] - out[8:16]
                count_tile = jnp.where(row8 == 2 * mm + r, out[16:24], count_tile)
        sums_ref[ch, 48:56, :] = count_tile
        return 0

    lax.fori_loop(0, CHUNKS, chunk, 0)


def local_totals(ids_row, rows, vectors, codes):
    return pl.pallas_call(
        totals_kernel,
        out_shape=(jax.ShapeDtypeStruct((CHUNKS, CHUNK_ROWS, CODES), F32),
                   jax.ShapeDtypeStruct((DIM, LANES), F32)),
        in_specs=[vmem()] * 4,
        out_specs=(vmem(), vmem()),
        scratch_shapes=[pltpu.VMEM((SUBS, 16, LANES), BF16)],
        compiler_params=pltpu.CompilerParams(vmem_limit_bytes=VMEM_LIMIT),
    )(ids_row, rows, vectors, codes)


def refit_kernel(sums_ref, book0_ref, book_ref, half, plane, line, plane_in, line_in,
                 core_send, core_recv, plane_send, plane_recv, line_send, line_recv,
                 unit_send, unit_recv, gather_send, gather_recv, back_send, back_recv):
    group, owner = place()
    x, core = group // 2, group % 2
    y, z = owner // 16, owner % 16
    xy = x * 4 + y
    sibling = group + 1 - 2 * core
    chunk = core * PLANE + xy

    def plane_device(i):
        return ((i // 4) * 2 + core, (i % 4) * 16 + z)

    barrier = pltpu.get_barrier_semaphore()
    pl.semaphore_signal(barrier, inc=1, device_id=(sibling, owner), device_id_type=MESH)
    for k in range(1, PLANE):
        pl.semaphore_signal(barrier, inc=1, device_id=plane_device((xy + k) % PLANE), device_id_type=MESH)
        pl.semaphore_signal(barrier, inc=1, device_id=(group, y * 16 + (z + k) % 16), device_id_type=MESH)
    pl.semaphore_wait(barrier, 1 + 2 * (PLANE - 1))

    def core_copy(k):
        i = (xy + 1 + k) % PLANE
        return pltpu.make_async_remote_copy(
            sums_ref.at[(1 - core) * PLANE + i], half.at[i], core_send.at[k], core_recv.at[k],
            device_id=(sibling, owner), device_id_type=MESH)

    def plane_copy(k):
        i = (xy + 1 + k) % PLANE
        return pltpu.make_async_remote_copy(
            plane.at[i], plane_in.at[xy], plane_send, plane_recv, device_id=plane_device(i), device_id_type=MESH)

    lax.fori_loop(0, PLANE, lambda k, _: (core_copy(k).start(), 0)[1], 0)

    def pass_on(k, _):
        i = (xy + 1 + k) % PLANE
        core_copy(k).wait_recv()
        plane[i] = sums_ref[core * PLANE + i] + half[i]

        @pl.when(k < PLANE - 1)
        def _():
            plane_copy(k).start()
        return 0

    lax.fori_loop(0, PLANE, pass_on, 0)
    plane_in[xy] = plane[xy]
    wait_bytes(plane.at[pl.ds(0, PLANE - 1)], plane_recv)
    for mm in range(CHUNK_SUBS):
        total = plane_in[0, 16 * mm: 16 * mm + 16, :]
        for i in range(1, PLANE):
            total = total + plane_in[i, 16 * mm: 16 * mm + 16, :]
        line[2 * mm, 0:16, :] = total[:, 0:128]
        line[2 * mm + 1, 0:16, :] = total[:, 128:256]
    total = plane_in[0, 48:56, :]
    for i in range(1, PLANE):
        total = total + plane_in[i, 48:56, :]
    for unit in range(6):
        side = unit % 2
        line[unit, 16:24, :] = total[:, 128 * side: 128 * side + 128]

    def line_copy(unit):
        return pltpu.make_async_remote_copy(
            line.at[unit], line_in.at[z], line_send.at[unit], line_recv,
            device_id=(group, y * 16 + UNIT_PLACES[unit]), device_id_type=MESH)

    for unit, where in enumerate(UNIT_PLACES):
        @pl.when(z != where)
        def _(unit=unit):
            line_copy(unit).start()

    def unit_ref(unit):
        mm, side = unit // 2, unit % 2
        return book_ref.at[chunk, 8 * mm: 8 * mm + 8, 128 * side: 128 * side + 128]

    def unit_copy(unit, k):
        return pltpu.make_async_remote_copy(
            unit_ref(unit), unit_ref(unit), unit_send, unit_recv.at[unit],
            device_id=(group, y * 16 + (z + k) % 16), device_id_type=MESH)

    for unit, where in enumerate(UNIT_PLACES):
        mm, side = unit // 2, unit % 2

        @pl.when(z == where)
        def _(unit=unit, mm=mm, side=side, where=where):
            line_in[where] = line[unit]
            wait_bytes(line_in.at[pl.ds(0, PLANE - 1)], line_recv)
            total = line_in[0]
            for i in range(1, PLANE):
                total = total + line_in[i]
            start = book0_ref[chunk, 8 * mm: 8 * mm + 8, 128 * side: 128 * side + 128]
            first = (total[0:8] + PRIOR * start) / (total[16 + 2 * mm: 17 + 2 * mm] + PRIOR)
            book_ref[chunk, 8 * mm: 8 * mm + 8, 128 * side: 128 * side + 128] = (
                (total[8:16] + PRIOR * first) / (total[17 + 2 * mm: 18 + 2 * mm] + PRIOR))
            lax.fori_loop(1, PLANE, lambda k, _: (unit_copy(unit, k).start(), 0)[1], 0)

    for unit, where in enumerate(UNIT_PLACES):
        @pl.when(z != where)
        def _(unit=unit):
            wait_bytes(unit_ref(unit), unit_recv.at[unit])

    def gather_copy(k):
        return pltpu.make_async_remote_copy(
            book_ref.at[chunk], book_ref.at[chunk], gather_send, gather_recv,
            device_id=plane_device((xy + k) % PLANE), device_id_type=MESH)

    lax.fori_loop(1, PLANE, lambda k, _: (gather_copy(k).start(), 0)[1], 0)
    wait_bytes(book_ref.at[pl.ds(0, PLANE - 1)], gather_recv)

    mine = book_ref.at[pl.ds(core * PLANE, PLANE)]
    back = pltpu.make_async_remote_copy(
        mine, mine, back_send, back_recv, device_id=(sibling, owner), device_id_type=MESH)
    back.start()

    lax.fori_loop(0, PLANE, lambda k, _: (core_copy(k).wait_send(), 0)[1], 0)
    wait_bytes(plane.at[pl.ds(0, PLANE - 1)], plane_send)
    for unit, where in enumerate(UNIT_PLACES):
        @pl.when(z != where)
        def _(unit=unit):
            line_copy(unit).wait_send()

        @pl.when(z == where)
        def _(unit=unit):
            def sent(k, _):
                unit_copy(unit, k).wait_send()
                return 0
            lax.fori_loop(1, PLANE, sent, 0)
    wait_bytes(book_ref.at[pl.ds(0, PLANE - 1)], gather_send)
    back.wait()


def refit(sums, book0):
    return pl.pallas_call(
        refit_kernel,
        out_shape=jax.ShapeDtypeStruct((CHUNKS, CHUNK_SUBS * WIDTH, CODES), F32),
        in_specs=[vmem()] * 2,
        out_specs=vmem(),
        scratch_shapes=[
            pltpu.VMEM((PLANE, CHUNK_ROWS, CODES), F32),
            pltpu.VMEM((PLANE, CHUNK_ROWS, CODES), F32),
            pltpu.VMEM((6, 24, LANES), F32),
            pltpu.VMEM((PLANE, CHUNK_ROWS, CODES), F32),
            pltpu.VMEM((PLANE, 24, LANES), F32),
            pltpu.SemaphoreType.DMA((PLANE,)), pltpu.SemaphoreType.DMA((PLANE,)),
            pltpu.SemaphoreType.DMA, pltpu.SemaphoreType.DMA,
            pltpu.SemaphoreType.DMA((6,)), pltpu.SemaphoreType.DMA,
            pltpu.SemaphoreType.DMA, pltpu.SemaphoreType.DMA((6,)),
            pltpu.SemaphoreType.DMA, pltpu.SemaphoreType.DMA,
            pltpu.SemaphoreType.DMA, pltpu.SemaphoreType.DMA,
        ],
        compiler_params=pltpu.CompilerParams(collective_id=1, has_side_effects=True, vmem_limit_bytes=VMEM_LIMIT),
    )(sums, book0)


def error_kernel(resid_ref, codes_ref, book_ref, key_ref, out_ref, mine, errors, parts, parts_in,
                 err_send, err_recv, part_send, part_recv):
    group, owner = place()
    barrier = pltpu.get_barrier_semaphore()

    def greet(k, _):
        pl.semaphore_signal(barrier, inc=1, device_id=(group, (owner + k) % OWNERS), device_id_type=MESH)
        return 0

    lax.fori_loop(1, OWNERS, greet, 0)
    for k in range(1, GROUPS):
        pl.semaphore_signal(barrier, inc=1, device_id=((group + k) % GROUPS, owner), device_id_type=MESH)

    def add(ch, total):
        for mm in range(CHUNK_SUBS):
            m = ch * CHUNK_SUBS + mm
            code = jnp.broadcast_to(codes_ref[pl.ds(SUBS + m, 1), :], (WIDTH, LANES))
            low = code & 127
            one = jnp.take_along_axis(book_ref[ch, 8 * mm: 8 * mm + 8, 0:128], low, axis=1)
            two = jnp.take_along_axis(book_ref[ch, 8 * mm: 8 * mm + 8, 128:256], low, axis=1)
            diff = resid_ref[pl.ds(8 * m, 8), :] - jnp.where(code > 127, two, one)
            total = total + diff * diff
        return total

    total = lax.fori_loop(0, CHUNKS, add, jnp.zeros((WIDTH, LANES), F32))
    mine[...] = jnp.sum(total, axis=0, keepdims=True) / float(DIM)
    pl.semaphore_wait(barrier, OWNERS - 1 + GROUPS - 1)

    def err_copy(k):
        return pltpu.make_async_remote_copy(
            mine, errors.at[owner], err_send, err_recv, device_id=(group, (owner + k) % OWNERS), device_id_type=MESH)

    lax.fori_loop(1, OWNERS, lambda k, _: (err_copy(k).start(), 0)[1], 0)
    errors[owner] = mine[...]
    wait_bytes(errors.at[pl.ds(0, OWNERS - 1)], err_recv)

    slot_base = lax.broadcasted_iota(I32, (OWNERS, SLOTS, LANES), 1).astype(F32) * 2048.0
    at = key_ref[...] - slot_base
    hit = (at > 0.5) & (at < 1024.5)
    which = jnp.sum(jnp.where(hit, at, 0.0), axis=2, keepdims=True).reshape(OWNERS * SLOTS, 1)
    value = jnp.sum(jnp.where(hit, jnp.broadcast_to(errors[...], hit.shape), 0.0), axis=2, keepdims=True)
    value = value.reshape(OWNERS * SLOTS, 1)
    lane = lax.broadcasted_iota(I32, (OWNERS * SLOTS, LANES), 1).astype(F32) + 1.0
    for block in range(GROUPS):
        chosen = jnp.where(which == lane + 128.0 * block, value, 0.0)
        parts[block] = jnp.sum(chosen, axis=0, keepdims=True)

    def part_copy(k):
        return pltpu.make_async_remote_copy(
            parts.at[(group + k) % GROUPS], parts_in.at[group], part_send, part_recv,
            device_id=((group + k) % GROUPS, owner), device_id_type=MESH)

    for k in range(1, GROUPS):
        part_copy(k).start()
    parts_in[group] = parts[group]
    wait_bytes(parts.at[pl.ds(0, GROUPS - 1)], part_recv)
    sum_here = parts_in[0]
    for i in range(1, GROUPS):
        sum_here = sum_here + parts_in[i]
    out_ref[...] = sum_here
    wait_bytes(parts.at[pl.ds(0, GROUPS - 1)], part_send)
    wait_bytes(errors.at[pl.ds(0, OWNERS - 1)], err_send)


def list_errors(resid, codes, book, key):
    return pl.pallas_call(
        error_kernel,
        out_shape=jax.ShapeDtypeStruct((1, LANES), F32),
        in_specs=[vmem()] * 4,
        out_specs=vmem(),
        scratch_shapes=[
            pltpu.VMEM((1, LANES), F32),
            pltpu.VMEM((OWNERS, 1, LANES), F32),
            pltpu.VMEM((GROUPS, 1, LANES), F32),
            pltpu.VMEM((GROUPS, 1, LANES), F32),
            pltpu.SemaphoreType.DMA, pltpu.SemaphoreType.DMA,
            pltpu.SemaphoreType.DMA, pltpu.SemaphoreType.DMA,
        ],
        compiler_params=pltpu.CompilerParams(collective_id=2, has_side_effects=True, vmem_limit_bytes=VMEM_LIMIT),
    )(resid, codes, book, key)


def local(vectors, list_ids, codes, centroids, codebook0):
    ids_row = list_ids.reshape(1, ROWS)
    rows, key = fetch_rows(ids_row, centroids)
    sums, resid = local_totals(ids_row, rows, vectors, codes)
    book = refit(sums, codebook0.reshape(CHUNKS, CHUNK_SUBS * WIDTH, CODES))
    list_error = list_errors(resid, codes, book, key)
    return book.reshape(SUBS, WIDTH, CODES), list_error.reshape(ROWS)


def solution(mesh):
    in_specs = (
        P(("groups", "owners"), None),
        P(("groups", "owners")),
        P(None, ("groups", "owners")),
        P(("groups", "owners"), None),
        P(),
    )
    out_specs = (P(), P(("groups", "owners")))
    return jax.shard_map(local, mesh=mesh, in_specs=in_specs, out_specs=out_specs, check_vma=False)
```

```python
import jax
import jax.numpy as jnp
from jax import lax
from jax.experimental import pallas as pl
from jax.experimental.pallas import tpu as pltpu
from jax.sharding import PartitionSpec as P

MESH = pl.DeviceIdType.MESH
F32 = jnp.float32
BF16 = jnp.bfloat16
I32 = jnp.int32

ROWS = 128
DIM = 768
SUBS = 96
WIDTH = 8
CODES = 256
OWNERS = 64
GROUPS = 8
CAP = 6
SLOTS = 8
LANES = 128
PAIRS = 3
LISTS_HERE = GROUPS * ROWS
CHUNKS = 32
CHUNK_SUBS = SUBS // CHUNKS
CHUNK_ROWS = 56
PLANE = 16
PRIOR = 128.0
UNIT_PLACES = (0, 2, 5, 8, 10, 13)
HELD = CAP * OWNERS
VMEM_LIMIT = 48 * 1024 * 1024


def vmem():
    return pl.BlockSpec(memory_space=pltpu.VMEM)


def wait_bytes(ref, sem):
    pltpu.make_async_copy(ref, ref, sem).wait()


def place():
    group, owner = lax.axis_index("groups"), lax.axis_index("owners")
    return group, owner


def local_copy(src, dst, sem):
    copy = pltpu.make_async_copy(src, dst, sem)
    copy.start()
    return copy


def each(first, last, body):
    def step(k, carry):
        body(k)
        return carry
    lax.fori_loop(first, last, step, 0)


def index_kernel(ids_hbm, vec_hbm, codes_hbm, cent_hbm, book0_hbm, book_ref, out_ref,
                 ids_v, vec_v, codes_v, book0_v, table, place_v, vec_t, vec_out, vec_in, code_out, code_in,
                 code_f, held_codes, pick_v, base_t, sums, half, plane, plane_in, line, line_in, parts, parts_in,
                 load_sem, code_send, code_recv, vec_send, vec_recv, x_send, x_recv, sib_send, sib_recv,
                 core_send, core_recv, plane_send, plane_recv, line_send, line_recv,
                 unit_send, unit_recv, gather_send, gather_recv, back_send, back_recv, part_send, part_recv):
    group, owner = place()
    x, core = group // 2, group % 2
    y, z = owner // 16, owner % 16
    xy = x * 4 + y
    sibling = group + 1 - 2 * core
    chunk = core * PLANE + xy

    def plane_device(i):
        return ((i // 4) * 2 + core, (i % 4) * 16 + z)

    barrier = pltpu.get_barrier_semaphore()
    each(1, OWNERS, lambda k: pl.semaphore_signal(
        barrier, inc=1, device_id=(group, (owner + k) % OWNERS), device_id_type=MESH))
    for k in range(1, GROUPS):
        pl.semaphore_signal(barrier, inc=1, device_id=((group + k) % GROUPS, owner), device_id_type=MESH)
    for i in range(1, 4):
        for j in range(1, 4):
            pl.semaphore_signal(
                barrier, inc=1, device_id=((group + 2 * i) % GROUPS, (owner + 16 * j) % OWNERS), device_id_type=MESH)

    load_ids = local_copy(ids_hbm, ids_v, load_sem.at[0])
    load_codes = local_copy(codes_hbm, codes_v, load_sem.at[1])
    load_vec = local_copy(vec_hbm, vec_v, load_sem.at[2])
    load_cent = local_copy(cent_hbm, table.at[group], load_sem.at[3])
    load_book = local_copy(book0_hbm.at[chunk], book0_v, load_sem.at[4])

    load_ids.wait()
    ids = ids_v[...]
    owner_of = (ids >> 7) & (OWNERS - 1)
    in_owner = (lax.broadcasted_iota(I32, (OWNERS, LANES), 0) == owner_of).astype(F32)
    before = (lax.broadcasted_iota(I32, (LANES, LANES), 0) < lax.broadcasted_iota(I32, (LANES, LANES), 1))
    running = jnp.dot(in_owner.astype(BF16), before.astype(F32).astype(BF16), preferred_element_type=F32)
    rank = jnp.sum(in_owner * running, axis=0, keepdims=True).astype(I32)
    slot = owner_of * SLOTS + rank
    place_v[...] = (lax.broadcasted_iota(I32, (OWNERS * SLOTS, LANES), 0) == slot).astype(F32).astype(BF16)
    list_no = ((ids >> 13) << 7) + (ids & 127) + 1

    def pack(rows):
        both = jnp.concatenate([rows[:, 0:128].reshape(OWNERS, SLOTS, LANES),
                                rows[:, 128:256].reshape(OWNERS, SLOTS, LANES)], axis=1)
        return both.astype(BF16)

    load_codes.wait()
    row8 = lax.broadcasted_iota(I32, (8, LANES), 0)
    list_rows = jnp.where(row8 == 0, list_no >> 8, jnp.where(row8 == 1, list_no & 255, 0)).astype(F32)
    load = jnp.concatenate(
        [codes_v[...].astype(F32), list_rows, jnp.zeros((CODES - 2 * SUBS - 8, LANES), F32)], axis=0).astype(BF16)
    code_out[...] = pack(lax.dot_general(
        place_v[...], load, (((1,), (1,)), ((), ())), preferred_element_type=F32))

    load_cent.wait()
    pl.semaphore_wait(barrier, OWNERS - 1 + GROUPS - 1 + 9)

    def code_copy(k):
        peer = (owner + k) % OWNERS
        return pltpu.make_async_remote_copy(
            code_out.at[peer], code_in.at[owner], code_send, code_recv, device_id=(group, peer), device_id_type=MESH)

    def vec_copy(k):
        peer = (owner + k) % OWNERS
        return pltpu.make_async_remote_copy(
            vec_out.at[peer], vec_in.at[owner], vec_send, vec_recv, device_id=(group, peer), device_id_type=MESH)

    across = []
    for j in range(1, 4):
        across.append(pltpu.make_async_remote_copy(
            table.at[group], table.at[group], x_send.at[j - 1], x_recv.at[j - 1],
            device_id=((group + 2 * j) % GROUPS, owner), device_id_type=MESH))
    aside = [pltpu.make_async_remote_copy(
        table.at[group], table.at[group], sib_send.at[0], sib_recv.at[0],
        device_id=(sibling, owner), device_id_type=MESH)]
    each(1, OWNERS, lambda k: code_copy(k).start())
    for copy in across + aside:
        copy.start()
    code_in[owner] = code_out[owner]

    load_vec.wait()
    for p in range(PAIRS):
        rows = jnp.dot(place_v[...], vec_v[:, 256 * p: 256 * p + 256], preferred_element_type=F32)
        vec_out[:, 16 * p: 16 * p + 16, :] = pack(rows)
        for h in range(2):
            j = 2 * p + h
            vec_t[128 * j: 128 * j + 128, :] = vec_v[:, 128 * j: 128 * j + 128].astype(F32).T
    vec_in[owner] = vec_out[owner]

    for j in range(1, 4):
        source = (group + 2 * GROUPS - 2 * j) % GROUPS
        across[j - 1].wait_recv()
        relay = pltpu.make_async_remote_copy(
            table.at[source], table.at[source], sib_send.at[j], sib_recv.at[j],
            device_id=(sibling, owner), device_id_type=MESH)
        relay.start()
        aside.append(relay)

    ones = jnp.ones((8, LANES), F32)
    tile_row = lax.broadcasted_iota(I32, (8, CODES), 0)
    level = lax.broadcasted_iota(I32, (CODES, LANES), 0)

    def vector_sums(ch):
        count_tile = jnp.zeros((8, CODES), F32)
        for mm in range(CHUNK_SUBS):
            m = ch * CHUNK_SUBS + mm
            left = jnp.concatenate([vec_t[pl.ds(8 * m, 8), :], ones], axis=0).astype(BF16)
            for r in range(2):
                onehot = (level == codes_v[pl.ds(r * SUBS + m, 1), :]).astype(F32).astype(BF16)
                out = lax.dot_general(left, onehot, (((1,), (1,)), ((), ())), preferred_element_type=F32)
                sums[ch, 16 * mm + 8 * r: 16 * mm + 8 * r + 8, :] = out[0:8]
                count_tile = jnp.where(tile_row == 2 * mm + r, out[8:16], count_tile)
        sums[ch, 48:56, :] = count_tile

    each(0, CHUNKS, vector_sums)

    wait_bytes(code_in.at[pl.ds(0, OWNERS - 1)], code_recv)
    each(1, OWNERS, lambda k: vec_copy(k).start())

    code_f[...] = code_in[...].astype(F32)
    for h in range(2):
        rows = jnp.concatenate([code_f[:, 8 * h + s, :] for s in range(CAP)], axis=0)
        held_codes[128 * h: 128 * h + 128, :] = rows.T.astype(I32)
        if h == 1:
            which = rows[:, 64:65] * 256.0 + rows[:, 65:66]
    lane = lax.broadcasted_iota(I32, (HELD, LISTS_HERE), 1).astype(F32) + 1.0
    pick_v[...] = (which == lane).astype(F32).astype(BF16)
    for copy in aside:
        copy.wait_recv()
    for j in range(6):
        lists = table[:, :, 128 * j: 128 * j + 128].reshape(LISTS_HERE, LANES)
        base_t[128 * j: 128 * j + 128, :] = jnp.dot(pick_v[...], lists, preferred_element_type=F32).T

    wide = lax.broadcasted_iota(I32, (CODES, HELD), 0)

    def centroid_sums(ch):
        for mm in range(CHUNK_SUBS):
            m = ch * CHUNK_SUBS + mm
            left = base_t[pl.ds(8 * m, 8), :].astype(BF16)
            for r in range(2):
                onehot = (wide == held_codes[pl.ds(r * SUBS + m, 1), :]).astype(F32).astype(BF16)
                out = lax.dot_general(left, onehot, (((1,), (1,)), ((), ())), preferred_element_type=F32)
                sums[ch, 16 * mm + 8 * r: 16 * mm + 8 * r + 8, :] -= out

    def core_copy(k):
        i = (xy + 1 + k) % PLANE
        return pltpu.make_async_remote_copy(
            sums.at[(1 - core) * PLANE + i], half.at[i], core_send.at[k], core_recv.at[k],
            device_id=(sibling, owner), device_id_type=MESH)

    def plane_copy(k):
        i = (xy + 1 + k) % PLANE
        return pltpu.make_async_remote_copy(
            plane.at[i], plane_in.at[xy], plane_send, plane_recv, device_id=plane_device(i), device_id_type=MESH)

    def other_half(k):
        centroid_sums((1 - core) * PLANE + (xy + 1 + k) % PLANE)
        core_copy(k).start()

    each(0, PLANE, other_half)

    def own_half(k):
        i = (xy + 1 + k) % PLANE
        centroid_sums(core * PLANE + i)
        core_copy(k).wait_recv()
        plane[i] = sums[core * PLANE + i] + half[i]

        @pl.when(k < PLANE - 1)
        def _():
            plane_copy(k).start()

    each(0, PLANE, own_half)
    plane_in[xy] = plane[xy]
    wait_bytes(plane.at[pl.ds(0, PLANE - 1)], plane_recv)
    for mm in range(CHUNK_SUBS):
        total = plane_in[0, 16 * mm: 16 * mm + 16, :]
        for i in range(1, PLANE):
            total = total + plane_in[i, 16 * mm: 16 * mm + 16, :]
        line[2 * mm, 0:16, :] = total[:, 0:128]
        line[2 * mm + 1, 0:16, :] = total[:, 128:256]
    total = plane_in[0, 48:56, :]
    for i in range(1, PLANE):
        total = total + plane_in[i, 48:56, :]
    for unit in range(6):
        side = unit % 2
        line[unit, 16:24, :] = total[:, 128 * side: 128 * side + 128]

    def line_copy(unit):
        return pltpu.make_async_remote_copy(
            line.at[unit], line_in.at[z], line_send.at[unit], line_recv,
            device_id=(group, y * 16 + UNIT_PLACES[unit]), device_id_type=MESH)

    for unit, where in enumerate(UNIT_PLACES):
        @pl.when(z != where)
        def _(unit=unit):
            line_copy(unit).start()

    def unit_ref(unit):
        mm, side = unit // 2, unit % 2
        return book_ref.at[chunk, 8 * mm: 8 * mm + 8, 128 * side: 128 * side + 128]

    def unit_copy(unit, k):
        return pltpu.make_async_remote_copy(
            unit_ref(unit), unit_ref(unit), unit_send, unit_recv.at[unit],
            device_id=(group, y * 16 + (z + k) % 16), device_id_type=MESH)

    load_book.wait()
    for unit, where in enumerate(UNIT_PLACES):
        mm, side = unit // 2, unit % 2

        @pl.when(z == where)
        def _(unit=unit, mm=mm, side=side, where=where):
            line_in[where] = line[unit]
            wait_bytes(line_in.at[pl.ds(0, PLANE - 1)], line_recv)
            total = line_in[0]
            for i in range(1, PLANE):
                total = total + line_in[i]
            start = book0_v[8 * mm: 8 * mm + 8, 128 * side: 128 * side + 128]
            first = (total[0:8] + PRIOR * start) / (total[16 + 2 * mm: 17 + 2 * mm] + PRIOR)
            book_ref[chunk, 8 * mm: 8 * mm + 8, 128 * side: 128 * side + 128] = (
                (total[8:16] + PRIOR * first) / (total[17 + 2 * mm: 18 + 2 * mm] + PRIOR))
            each(1, PLANE, lambda k: unit_copy(unit, k).start())

    wait_bytes(vec_in.at[pl.ds(0, OWNERS - 1)], vec_recv)
    for p in range(PAIRS):
        code_f[...] = vec_in[:, 16 * p: 16 * p + 16, :].astype(F32)
        for h in range(2):
            j = 2 * p + h
            rows = jnp.concatenate([code_f[:, 8 * h + s, :] for s in range(CAP)], axis=0)
            base_t[128 * j: 128 * j + 128, :] = rows.T - base_t[128 * j: 128 * j + 128, :]

    for unit, where in enumerate(UNIT_PLACES):
        @pl.when(z != where)
        def _(unit=unit):
            wait_bytes(unit_ref(unit), unit_recv.at[unit])

    def gather_copy(k):
        return pltpu.make_async_remote_copy(
            book_ref.at[chunk], book_ref.at[chunk], gather_send, gather_recv,
            device_id=plane_device((xy + k) % PLANE), device_id_type=MESH)

    each(1, PLANE, lambda k: gather_copy(k).start())
    wait_bytes(book_ref.at[pl.ds(0, PLANE - 1)], gather_recv)

    mine = book_ref.at[pl.ds(core * PLANE, PLANE)]
    back = pltpu.make_async_remote_copy(
        mine, mine, back_send, back_recv, device_id=(sibling, owner), device_id_type=MESH)
    back.start()

    def add(ch, totals):
        for mm in range(CHUNK_SUBS):
            m = ch * CHUNK_SUBS + mm
            left = book_ref[ch, 8 * mm: 8 * mm + 8, 0:128]
            right = book_ref[ch, 8 * mm: 8 * mm + 8, 128:256]
            row = jnp.broadcast_to(held_codes[pl.ds(SUBS + m, 1), :], (WIDTH, HELD))
            new = []
            for t in range(HELD // LANES):
                code = row[:, 128 * t: 128 * t + 128]
                low = code & 127
                one = jnp.take_along_axis(left, low, axis=1)
                two = jnp.take_along_axis(right, low, axis=1)
                diff = base_t[pl.ds(8 * m, 8), 128 * t: 128 * t + 128] - jnp.where(code > 127, two, one)
                new.append(totals[t] + diff * diff)
            totals = tuple(new)
        return totals

    zero = jnp.zeros((WIDTH, LANES), F32)
    totals = lax.fori_loop(core * PLANE, core * PLANE + PLANE, add, (zero,) * 3)
    back.wait_recv()
    totals = lax.fori_loop((1 - core) * PLANE, (1 - core) * PLANE + PLANE, add, totals)
    error = jnp.concatenate([jnp.sum(t, axis=0, keepdims=True) for t in totals], axis=1) / float(DIM)
    top = error.astype(BF16).astype(F32)
    mid = (error - top).astype(BF16).astype(F32)
    low = error - top - mid
    row = lax.broadcasted_iota(I32, (16, HELD), 0)
    split = jnp.where(row == 0, top, jnp.where(row == 1, mid, jnp.where(row == 2, low, 0.0))).astype(BF16)
    by_list = jnp.sum(jnp.dot(split, pick_v[...], preferred_element_type=F32), axis=0, keepdims=True)
    for i in range(GROUPS):
        parts[i] = by_list[:, 128 * i: 128 * i + 128]

    def part_copy(k):
        return pltpu.make_async_remote_copy(
            parts.at[(group + k) % GROUPS], parts_in.at[group], part_send, part_recv,
            device_id=((group + k) % GROUPS, owner), device_id_type=MESH)

    for k in range(1, GROUPS):
        part_copy(k).start()
    parts_in[group] = parts[group]

    wait_bytes(code_in.at[pl.ds(0, OWNERS - 1)], code_send)
    wait_bytes(vec_in.at[pl.ds(0, OWNERS - 1)], vec_send)
    for copy in across + aside:
        copy.wait_send()
    each(0, PLANE, lambda k: core_copy(k).wait_send())
    wait_bytes(plane.at[pl.ds(0, PLANE - 1)], plane_send)
    for unit, where in enumerate(UNIT_PLACES):
        @pl.when(z != where)
        def _(unit=unit):
            line_copy(unit).wait_send()

        @pl.when(z == where)
        def _(unit=unit):
            each(1, PLANE, lambda k: unit_copy(unit, k).wait_send())
    wait_bytes(book_ref.at[pl.ds(0, PLANE - 1)], gather_send)
    back.wait_send()

    wait_bytes(parts.at[pl.ds(0, GROUPS - 1)], part_recv)
    sum_here = parts_in[0]
    for i in range(1, GROUPS):
        sum_here = sum_here + parts_in[i]
    out_ref[...] = sum_here
    wait_bytes(parts.at[pl.ds(0, GROUPS - 1)], part_send)


def local(vectors, list_ids, codes, centroids, codebook0):
    dma = pltpu.SemaphoreType.DMA
    any_place = pl.BlockSpec(memory_space=pl.ANY)
    book, list_error = pl.pallas_call(
        index_kernel,
        out_shape=(jax.ShapeDtypeStruct((CHUNKS, CHUNK_SUBS * WIDTH, CODES), F32),
                   jax.ShapeDtypeStruct((1, LANES), F32)),
        in_specs=[any_place] * 5,
        out_specs=(vmem(), vmem()),
        scratch_shapes=[
            pltpu.VMEM((1, LANES), I32),
            pltpu.VMEM((ROWS, DIM), BF16),
            pltpu.VMEM((2 * SUBS, LANES), I32),
            pltpu.VMEM((CHUNK_SUBS * WIDTH, CODES), F32),
            pltpu.VMEM((GROUPS, ROWS, DIM), BF16),
            pltpu.VMEM((OWNERS * SLOTS, LANES), BF16),
            pltpu.VMEM((DIM, LANES), F32),
            pltpu.VMEM((OWNERS, 16 * PAIRS, LANES), BF16),
            pltpu.VMEM((OWNERS, 16 * PAIRS, LANES), BF16),
            pltpu.VMEM((OWNERS, 16, LANES), BF16),
            pltpu.VMEM((OWNERS, 16, LANES), BF16),
            pltpu.VMEM((OWNERS, 16, LANES), F32),
            pltpu.VMEM((CODES, HELD), I32),
            pltpu.VMEM((HELD, LISTS_HERE), BF16),
            pltpu.VMEM((DIM, HELD), F32),
            pltpu.VMEM((CHUNKS, CHUNK_ROWS, CODES), F32),
            pltpu.VMEM((PLANE, CHUNK_ROWS, CODES), F32),
            pltpu.VMEM((PLANE, CHUNK_ROWS, CODES), F32),
            pltpu.VMEM((PLANE, CHUNK_ROWS, CODES), F32),
            pltpu.VMEM((6, 24, LANES), F32),
            pltpu.VMEM((PLANE, 24, LANES), F32),
            pltpu.VMEM((GROUPS, 1, LANES), F32),
            pltpu.VMEM((GROUPS, 1, LANES), F32),
            dma((5,)),
            dma, dma, dma, dma,
            dma((3,)), dma((3,)), dma((4,)), dma((4,)),
            dma((PLANE,)), dma((PLANE,)),
            dma, dma,
            dma((6,)), dma,
            dma, dma((6,)),
            dma, dma, dma, dma, dma, dma,
        ],
        compiler_params=pltpu.CompilerParams(collective_id=0, has_side_effects=True, vmem_limit_bytes=VMEM_LIMIT),
    )(list_ids.reshape(1, ROWS), vectors, codes, centroids,
      codebook0.reshape(CHUNKS, CHUNK_SUBS * WIDTH, CODES))
    return book.reshape(SUBS, WIDTH, CODES), list_error.reshape(ROWS)


def solution(mesh):
    in_specs = (
        P(("groups", "owners"), None),
        P(("groups", "owners")),
        P(None, ("groups", "owners")),
        P(("groups", "owners"), None),
        P(),
    )
    out_specs = (P(), P(("groups", "owners")))
    return jax.shard_map(local, mesh=mesh, in_specs=in_specs, out_specs=out_specs, check_vma=False)
```

```python
import jax
import jax.numpy as jnp
from jax import lax
from jax.experimental import pallas as pl
from jax.experimental.pallas import tpu as pltpu
from jax.sharding import PartitionSpec as P

MESH = pl.DeviceIdType.MESH
F32 = jnp.float32
BF16 = jnp.bfloat16
I32 = jnp.int32

ROWS = 128
DIM = 768
SUBS = 96
WIDTH = 8
CODES = 256
OWNERS = 64
GROUPS = 8
CAP = 6
SLOTS = 8
LANES = 128
PAIRS = 2
LISTS_HERE = GROUPS * ROWS
CHUNKS = 32
CHUNK_SUBS = SUBS // CHUNKS
CHUNK_ROWS = 2 * CHUNK_SUBS * WIDTH
PLANE = 16
PRIOR = 128.0
UNIT_PLACES = (0, 2, 5, 8, 10, 13)
VEC_FIRST = 28
HELD = CAP * OWNERS
VMEM_LIMIT = 60 * 1024 * 1024


def vmem():
    return pl.BlockSpec(memory_space=pltpu.VMEM)


def wait_bytes(ref, sem):
    pltpu.make_async_copy(ref, ref, sem).wait()


def place():
    group, owner = lax.axis_index("groups"), lax.axis_index("owners")
    return group, owner


def local_copy(src, dst, sem):
    copy = pltpu.make_async_copy(src, dst, sem)
    copy.start()
    return copy


def each(first, last, body):
    def step(k, carry):
        body(k)
        return carry
    lax.fori_loop(first, last, step, 0)


def index_kernel(ids_hbm, vec_hbm, codes_hbm, cent_hbm, book0_hbm, book_ref, out_ref,
                 ids_v, vec_v, codes_v, book0_v, table, place_v, spare_v, vec_t, vec_out, vec_in, code_out, code_in,
                 code_f, spare_f, held_codes, pick_v, base_t, sums, half, plane, plane_in, line, line_in, parts, parts_in,
                 tally, tally_half, tally_plane, tally_plane_in, tally_line, tally_line_in,
                 load_sem, code_send, code_recv, vec_send, vec_recv, x_send, x_recv, sib_send, sib_recv,
                 core_send, core_recv, plane_send, plane_recv, line_send, line_recv,
                 unit_send, unit_recv, gather_send, gather_recv, back_send, back_recv, part_send, part_recv,
                 t_core_send, t_core_recv, t_plane_send, t_plane_recv, t_line_send, t_line_recv):
    group, owner = place()
    x, core = group // 2, group % 2
    y, z = owner // 16, owner % 16
    xy = x * 4 + y
    sibling = group + 1 - 2 * core
    chunk = core * PLANE + xy

    def plane_device(i):
        return ((i // 4) * 2 + core, (i % 4) * 16 + z)

    def plane_to(k):
        step = (7 * k) % PLANE
        return (x + step // 4) % 4 * 4 + (y + step % 4) % 4

    def plane_from(k):
        step = (7 * k) % PLANE
        return (x + 4 - step // 4) % 4 * 4 + (y + 4 - step % 4) % 4

    def far_first(j):
        return (8 + (1 - 2 * (j % 2)) * ((j + 1) // 2)) % 16

    load_ids = local_copy(ids_hbm, ids_v, load_sem.at[0])
    load_codes = local_copy(codes_hbm, codes_v, load_sem.at[1])
    load_vec = local_copy(vec_hbm, vec_v, load_sem.at[2])
    load_cent = local_copy(cent_hbm, table.at[group], load_sem.at[3])
    load_book = local_copy(book0_hbm.at[chunk], book0_v, load_sem.at[4])

    barrier = pltpu.get_barrier_semaphore()

    def nth_peer(k):
        return (y + 3 - k % 4) % 4 * 16 + (z + far_first(k // 4)) % 16

    each(0, OWNERS - 1, lambda k: pl.semaphore_signal(
        barrier, inc=1, device_id=(group, nth_peer(k)), device_id_type=MESH))
    for k in range(1, GROUPS):
        pl.semaphore_signal(barrier, inc=1, device_id=((group + k) % GROUPS, owner), device_id_type=MESH)
    for i in range(1, 4):
        for j in range(1, 4):
            pl.semaphore_signal(
                barrier, inc=1, device_id=((group + 2 * i) % GROUPS, (owner + 16 * j) % OWNERS), device_id_type=MESH)

    load_ids.wait()
    ids = ids_v[...]
    owner_of = (ids >> 7) & (OWNERS - 1)
    in_owner = (lax.broadcasted_iota(I32, (OWNERS, LANES), 0) == owner_of).astype(F32)
    before = (lax.broadcasted_iota(I32, (LANES, LANES), 0) < lax.broadcasted_iota(I32, (LANES, LANES), 1))
    running = jnp.dot(in_owner.astype(BF16), before.astype(F32).astype(BF16), preferred_element_type=F32)
    rank = jnp.sum(in_owner * running, axis=0, keepdims=True).astype(I32)
    slot = owner_of * SLOTS + rank
    place_v[...] = (lax.broadcasted_iota(I32, (OWNERS * SLOTS, LANES), 0) == slot).astype(F32).astype(BF16)
    for q in range(3):
        here = jnp.where((rank >> 1) == q, slot + 6 - 2 * q, -1)
        spare_v[q] = (lax.broadcasted_iota(I32, (OWNERS * SLOTS, LANES), 0) == here).astype(F32).astype(BF16)
    list_no = ((ids >> 13) << 7) + (ids & 127) + 1

    def extra(part):
        block = 4 + part // 3
        return jnp.dot(spare_v[part % 3], vec_v[:, 128 * block: 128 * block + 128], preferred_element_type=F32)

    def pack(one, two):
        return jnp.concatenate([one.reshape(OWNERS, SLOTS, LANES), two.reshape(OWNERS, SLOTS, LANES)],
                               axis=1).astype(BF16)

    load_codes.wait()
    load_vec.wait()
    row8 = lax.broadcasted_iota(I32, (8, LANES), 0)
    list_rows = jnp.where(row8 == 0, list_no >> 8, jnp.where(row8 == 1, list_no & 255, 0)).astype(F32)
    load = jnp.concatenate(
        [codes_v[...].astype(F32), list_rows, jnp.zeros((CODES - 2 * SUBS - 8, LANES), F32)], axis=0).astype(BF16)
    rows = lax.dot_general(place_v[...], load, (((1,), (1,)), ((), ())), preferred_element_type=F32)
    code_out[...] = pack(rows[:, 0:128] + extra(0), rows[:, 128:256] + extra(1))

    load_cent.wait()
    pl.semaphore_wait(barrier, OWNERS - 1 + GROUPS - 1 + 9)

    def code_copy(k):
        peer = nth_peer(k)
        return pltpu.make_async_remote_copy(
            code_out.at[peer], code_in.at[owner], code_send, code_recv, device_id=(group, peer), device_id_type=MESH)

    def vec_copy(k):
        peer = nth_peer(k)
        return pltpu.make_async_remote_copy(
            vec_out.at[peer], vec_in.at[owner], vec_send, vec_recv, device_id=(group, peer), device_id_type=MESH)

    across = []
    for j in range(1, 4):
        across.append(pltpu.make_async_remote_copy(
            table.at[group], table.at[group], x_send.at[j - 1], x_recv.at[j - 1],
            device_id=((group + 2 * j) % GROUPS, owner), device_id_type=MESH))
    aside = [pltpu.make_async_remote_copy(
        table.at[group], table.at[group], sib_send.at[0], sib_recv.at[0],
        device_id=(sibling, owner), device_id_type=MESH)]
    each(0, OWNERS - 1, lambda k: code_copy(k).start())
    for copy in across + aside:
        copy.start()
    code_in[owner] = code_out[owner]

    for p in range(PAIRS):
        rows = jnp.dot(place_v[...], vec_v[:, 256 * p: 256 * p + 256], preferred_element_type=F32)
        vec_out[:, 16 * p: 16 * p + 16, :] = pack(
            rows[:, 0:128] + extra(2 + 2 * p), rows[:, 128:256] + extra(3 + 2 * p))
    vec_in[owner] = vec_out[owner]
    left_half = lax.broadcasted_iota(I32, (WIDTH, LANES), 1) < 64

    def by_code(pairs):
        lefts, rights = [], []
        low_level = lax.broadcasted_iota(I32, (64, pairs[0][1].shape[1]), 0)
        for rows, code in pairs:
            high = code >> 6
            lefts += [jnp.where(high == h, rows, 0.0) for h in range(4)]
            rights.append((low_level == (code & 63)).astype(F32))
        out = lax.dot_general(
            jnp.concatenate(lefts, axis=0).astype(BF16), jnp.concatenate(rights, axis=0).astype(BF16),
            (((1,), (1,)), ((), ())), preferred_element_type=F32)
        results = []
        for q in range(4):
            column = 128 * (q // 2)
            tiles = []
            for t in range(2):
                one = out[32 * q + 16 * t: 32 * q + 16 * t + 8, column: column + 128]
                two = out[32 * q + 16 * t + 8: 32 * q + 16 * t + 16, column: column + 128]
                if q % 2 == 0:
                    two = pltpu.roll(two, 64, 1)
                else:
                    one = pltpu.roll(one, 64, 1)
                tiles.append(jnp.where(left_half, one, two))
            results.append(jnp.concatenate(tiles, axis=1))
        return results

    def pairs_of(chunks):
        return [(ch, mm, r) for ch in chunks for mm in range(CHUNK_SUBS) for r in range(2)]

    ones = jnp.ones((WIDTH, LANES), F32)
    tile_row = lax.broadcasted_iota(I32, (8, CODES), 0)

    def count(c):
        pairs = pairs_of([2 * c, 2 * c + 1])
        tiles = [jnp.zeros((8, CODES), F32)] * 2
        for first in range(0, len(pairs), 4):
            four = pairs[first: first + 4]
            got = by_code([(ones, codes_v[pl.ds(r * SUBS + ch * CHUNK_SUBS + mm, 1), :]) for ch, mm, r in four])
            for n, (ch, mm, r) in enumerate(four):
                at = (first + n) // 6
                tiles[at] = jnp.where(tile_row == r * CHUNK_SUBS + mm, got[n], tiles[at])
        tally[2 * c] = tiles[0]
        tally[2 * c + 1] = tiles[1]

    each(0, CHUNKS // 2, count)

    t_core = pltpu.make_async_remote_copy(
        tally.at[pl.ds((1 - core) * PLANE, PLANE)], tally_half, t_core_send, t_core_recv,
        device_id=(sibling, owner), device_id_type=MESH)
    t_core.start()
    for j in range(6):
        vec_t[128 * j: 128 * j + 128, :] = vec_v[:, 128 * j: 128 * j + 128].astype(F32).T

    def t_plane_copy(k):
        i = plane_to(k)
        return pltpu.make_async_remote_copy(
            tally_plane.at[i], tally_plane_in.at[xy], t_plane_send, t_plane_recv,
            device_id=plane_device(i), device_id_type=MESH)

    def t_line_copy(unit):
        return pltpu.make_async_remote_copy(
            tally_line.at[unit % 2], tally_line_in.at[z], t_line_send.at[unit], t_line_recv,
            device_id=(group, y * 16 + UNIT_PLACES[unit]), device_id_type=MESH)

    def vector_sums(c):
        pairs = pairs_of([2 * c, 2 * c + 1])
        for first in range(0, len(pairs), 4):
            four = pairs[first: first + 4]
            got = by_code([(vec_t[pl.ds(8 * (ch * CHUNK_SUBS + mm), 8), :],
                            codes_v[pl.ds(r * SUBS + ch * CHUNK_SUBS + mm, 1), :]) for ch, mm, r in four])
            for n, (ch, mm, r) in enumerate(four):
                sums[ch, 16 * mm + 8 * r: 16 * mm + 8 * r + 8, :] = got[n]

    def total_of(ref):
        total = ref[0]
        for i in range(1, PLANE):
            total = total + ref[i]
        return total

    each(0, CHUNKS // 4, vector_sums)
    t_core.wait_recv()
    tally_plane[...] = tally[pl.ds(core * PLANE, PLANE)] + tally_half[...]
    each(1, PLANE, lambda k: t_plane_copy(k).start())
    tally_plane_in[xy] = tally_plane[xy]
    for j in range(1, 4):
        source = (group + 2 * GROUPS - 2 * j) % GROUPS
        across[j - 1].wait_recv()
        relay = pltpu.make_async_remote_copy(
            table.at[source], table.at[source], sib_send.at[j], sib_recv.at[j],
            device_id=(sibling, owner), device_id_type=MESH)
        relay.start()
        aside.append(relay)
    each(CHUNKS // 4, CHUNKS // 2, vector_sums)
    wait_bytes(tally_plane.at[pl.ds(0, PLANE - 1)], t_plane_recv)
    total = total_of(tally_plane_in)
    tally_line[0] = total[:, 0:128]
    tally_line[1] = total[:, 128:256]
    for unit, where in enumerate(UNIT_PLACES):
        @pl.when(z != where)
        def _(unit=unit):
            t_line_copy(unit).start()
    each(0, VEC_FIRST, lambda k: vec_copy(k).start())

    wait_bytes(code_in.at[pl.ds(0, OWNERS - 1)], code_recv)

    code_f[...] = code_in[...].astype(F32)
    for h in range(2):
        rows = jnp.concatenate([code_f[:, 8 * h + s, :] for s in range(CAP)], axis=0)
        held_codes[128 * h: 128 * h + 128, :] = rows.T.astype(I32)
        if h == 1:
            which = rows[:, 64:65] * 256.0 + rows[:, 65:66]
    lane = lax.broadcasted_iota(I32, (HELD, LISTS_HERE), 1).astype(F32) + 1.0
    pick_v[...] = (which == lane).astype(F32).astype(BF16)
    for copy in aside:
        copy.wait_recv()
    rows = jnp.dot(pick_v[...], table[...].reshape(LISTS_HERE, DIM), preferred_element_type=F32)
    for j in range(6):
        base_t[128 * j: 128 * j + 128, :] = rows[:, 128 * j: 128 * j + 128].T

    def centroid_sums(chunks):
        pairs = pairs_of(chunks)
        for first in range(0, len(pairs), 4):
            four = pairs[first: first + 4]
            got = by_code([(base_t[pl.ds(8 * (ch * CHUNK_SUBS + mm), 8), :],
                            held_codes[pl.ds(r * SUBS + ch * CHUNK_SUBS + mm, 1), :]) for ch, mm, r in four])
            for n, (ch, mm, r) in enumerate(four):
                sums[ch, 16 * mm + 8 * r: 16 * mm + 8 * r + 8, :] -= got[n]

    def core_copy(k):
        i = plane_to(k + 1)
        return pltpu.make_async_remote_copy(
            sums.at[(1 - core) * PLANE + i], half.at[i], core_send.at[k], core_recv.at[k],
            device_id=(sibling, owner), device_id_type=MESH)

    def plane_copy(k):
        i = plane_to(k + 1)
        return pltpu.make_async_remote_copy(
            plane.at[i], plane_in.at[xy], plane_send, plane_recv, device_id=plane_device(i), device_id_type=MESH)

    def other_half(c):
        k = 2 * c
        centroid_sums([(1 - core) * PLANE + plane_to(k + 1), (1 - core) * PLANE + plane_to(k + 2)])
        core_copy(k).start()
        core_copy(k + 1).start()

    def own_half(c):
        k = 2 * c
        centroid_sums([core * PLANE + plane_to(k + 1), core * PLANE + plane_to(k + 2)])
        for n in (k, k + 1):
            i = plane_to(n + 1)
            core_copy(n).wait_recv()
            plane[i] = sums[core * PLANE + i] + half[i]

            @pl.when(n < PLANE - 1)
            def _(n=n):
                plane_copy(n).start()

    def both_halves(c):
        @pl.when(c < PLANE // 2)
        def _():
            other_half(c)

        @pl.when(c > 0)
        def _():
            own_half(c - 1)

    each(0, PLANE // 2 + 1, both_halves)
    plane_in[xy] = plane[xy]
    wait_bytes(plane.at[pl.ds(0, PLANE - 1)], plane_recv)
    total = total_of(plane_in)
    for unit in range(6):
        mm, side = unit // 2, unit % 2
        line[unit] = total[16 * mm: 16 * mm + 16, 128 * side: 128 * side + 128]

    def line_copy(unit):
        return pltpu.make_async_remote_copy(
            line.at[unit], line_in.at[z], line_send.at[unit], line_recv,
            device_id=(group, y * 16 + UNIT_PLACES[unit]), device_id_type=MESH)

    for unit, where in enumerate(UNIT_PLACES):
        @pl.when(z != where)
        def _(unit=unit):
            line_copy(unit).start()

    each(VEC_FIRST, OWNERS - 1, lambda k: vec_copy(k).start())

    def unit_ref(unit):
        mm, side = unit // 2, unit % 2
        return book_ref.at[chunk, 8 * mm: 8 * mm + 8, 128 * side: 128 * side + 128]

    def unit_copy(unit, k):
        return pltpu.make_async_remote_copy(
            unit_ref(unit), unit_ref(unit), unit_send, unit_recv.at[unit],
            device_id=(group, y * 16 + (z + far_first(k)) % 16), device_id_type=MESH)

    load_book.wait()
    for unit, where in enumerate(UNIT_PLACES):
        mm, side = unit // 2, unit % 2

        @pl.when(z == where)
        def _(unit=unit, mm=mm, side=side, where=where):
            line_in[where] = line[unit]
            tally_line_in[where] = tally_line[side]
            wait_bytes(tally_line_in.at[pl.ds(0, PLANE - 1)], t_line_recv)
            counts = total_of(tally_line_in)
            wait_bytes(line_in.at[pl.ds(0, PLANE - 1)], line_recv)
            total = total_of(line_in)
            here = slice(128 * side, 128 * side + 128)
            start = book0_v[8 * mm: 8 * mm + 8, here]
            first = (total[0:8] + PRIOR * start) / (counts[mm: mm + 1] + PRIOR)
            book_ref[chunk, 8 * mm: 8 * mm + 8, here] = (
                (total[8:16] + PRIOR * first) / (counts[3 + mm: 4 + mm] + PRIOR))
            each(0, PLANE - 1, lambda k: unit_copy(unit, k).start())

    for unit, where in enumerate(UNIT_PLACES):
        @pl.when(z != where)
        def _(unit=unit):
            wait_bytes(unit_ref(unit), unit_recv.at[unit])

    def gather_copy(k):
        return pltpu.make_async_remote_copy(
            book_ref.at[chunk], book_ref.at[chunk], gather_send, gather_recv.at[k],
            device_id=plane_device(plane_to(k)), device_id_type=MESH)

    def back_copy(k):
        part = book_ref.at[core * PLANE + plane_from(k)]
        return pltpu.make_async_remote_copy(
            part, part, back_send, back_recv.at[k], device_id=(sibling, owner), device_id_type=MESH)

    each(1, PLANE, lambda k: gather_copy(k).start())
    back_copy(0).start()

    def take_spare(part):
        for h in range(2):
            for i in range(2):
                t = 2 * (part + h) + i
                spare_f[OWNERS * t: OWNERS * t + OWNERS, :] = code_f[:, 8 * h + 6 + i, :]

    code_f[...] = code_in[...].astype(F32)
    take_spare(0)
    wait_bytes(vec_in.at[pl.ds(0, OWNERS - 1)], vec_recv)
    for p in range(PAIRS):
        code_f[...] = vec_in[:, 16 * p: 16 * p + 16, :].astype(F32)
        take_spare(2 + 2 * p)
        for h in range(2):
            j = 2 * p + h
            rows = jnp.concatenate([code_f[:, 8 * h + s, :] for s in range(CAP)], axis=0)
            base_t[128 * j: 128 * j + 128, :] = rows.T - base_t[128 * j: 128 * j + 128, :]
    for j in range(4, 6):
        rows = spare_f[HELD * (j - 4): HELD * (j - 4) + HELD, :]
        base_t[128 * j: 128 * j + 128, :] = rows.T - base_t[128 * j: 128 * j + 128, :]

    def add(ch, totals):
        for mm in range(CHUNK_SUBS):
            m = ch * CHUNK_SUBS + mm
            left = book_ref[ch, 8 * mm: 8 * mm + 8, 0:128]
            right = book_ref[ch, 8 * mm: 8 * mm + 8, 128:256]
            row = jnp.broadcast_to(held_codes[pl.ds(SUBS + m, 1), :], (WIDTH, HELD))
            rest = base_t[pl.ds(8 * m, 8), :]
            new = []
            for t in range(HELD // LANES):
                code = row[:, 128 * t: 128 * t + 128]
                low = code & 127
                one = jnp.take_along_axis(left, low, axis=1)
                two = jnp.take_along_axis(right, low, axis=1)
                diff = rest[:, 128 * t: 128 * t + 128] - jnp.where(code > 127, two, one)
                new.append(totals[t] + diff * diff)
            totals = tuple(new)
        return totals

    def arrivals(k, totals):
        i = plane_from(k)
        part = book_ref.at[core * PLANE + i]
        wait_bytes(part, gather_recv.at[k])
        back_copy(k).start()
        before_it = (1 - core) * PLANE + plane_from(k - 1)
        wait_bytes(part, back_recv.at[k - 1])
        return add(before_it, add(core * PLANE + i, totals))

    zero = jnp.zeros((WIDTH, LANES), F32)
    totals = add(chunk, (zero,) * 3)
    totals = lax.fori_loop(1, PLANE, arrivals, totals)
    wait_bytes(book_ref.at[0], back_recv.at[PLANE - 1])
    totals = add((1 - core) * PLANE + plane_from(PLANE - 1), totals)
    error = jnp.concatenate([jnp.sum(t, axis=0, keepdims=True) for t in totals], axis=1) / float(DIM)
    top = error.astype(BF16).astype(F32)
    mid = (error - top).astype(BF16).astype(F32)
    low = error - top - mid
    row = lax.broadcasted_iota(I32, (16, HELD), 0)
    split = jnp.where(row == 0, top, jnp.where(row == 1, mid, jnp.where(row == 2, low, 0.0))).astype(BF16)
    by_list = jnp.sum(jnp.dot(split, pick_v[...], preferred_element_type=F32), axis=0, keepdims=True)
    for i in range(GROUPS):
        parts[i] = by_list[:, 128 * i: 128 * i + 128]

    def part_copy(k):
        return pltpu.make_async_remote_copy(
            parts.at[(group + k) % GROUPS], parts_in.at[group], part_send, part_recv,
            device_id=((group + k) % GROUPS, owner), device_id_type=MESH)

    for k in range(1, GROUPS):
        part_copy(k).start()
    parts_in[group] = parts[group]

    t_core.wait_send()
    wait_bytes(tally_plane.at[pl.ds(0, PLANE - 1)], t_plane_send)
    wait_bytes(code_in.at[pl.ds(0, OWNERS - 1)], code_send)
    wait_bytes(vec_in.at[pl.ds(0, OWNERS - 1)], vec_send)
    for copy in across + aside:
        copy.wait_send()
    each(0, PLANE, lambda k: core_copy(k).wait_send())
    wait_bytes(plane.at[pl.ds(0, PLANE - 1)], plane_send)
    for unit, where in enumerate(UNIT_PLACES):
        @pl.when(z != where)
        def _(unit=unit):
            line_copy(unit).wait_send()
            t_line_copy(unit).wait_send()

        @pl.when(z == where)
        def _(unit=unit):
            each(0, PLANE - 1, lambda k: unit_copy(unit, k).wait_send())
    wait_bytes(book_ref.at[pl.ds(0, PLANE - 1)], gather_send)
    wait_bytes(book_ref.at[pl.ds(0, PLANE)], back_send)

    wait_bytes(parts.at[pl.ds(0, GROUPS - 1)], part_recv)
    sum_here = parts_in[0]
    for i in range(1, GROUPS):
        sum_here = sum_here + parts_in[i]
    out_ref[...] = sum_here
    wait_bytes(parts.at[pl.ds(0, GROUPS - 1)], part_send)


def local(vectors, list_ids, codes, centroids, codebook0):
    dma = pltpu.SemaphoreType.DMA
    any_place = pl.BlockSpec(memory_space=pltpu.HBM)
    book, list_error = pl.pallas_call(
        index_kernel,
        out_shape=(jax.ShapeDtypeStruct((CHUNKS, CHUNK_SUBS * WIDTH, CODES), F32),
                   jax.ShapeDtypeStruct((1, LANES), F32)),
        in_specs=[any_place] * 5,
        out_specs=(vmem(), vmem()),
        scratch_shapes=[
            pltpu.VMEM((1, LANES), I32),
            pltpu.VMEM((ROWS, DIM), BF16),
            pltpu.VMEM((2 * SUBS, LANES), I32),
            pltpu.VMEM((CHUNK_SUBS * WIDTH, CODES), F32),
            pltpu.VMEM((GROUPS, ROWS, DIM), BF16),
            pltpu.VMEM((OWNERS * SLOTS, LANES), BF16),
            pltpu.VMEM((3, OWNERS * SLOTS, LANES), BF16),
            pltpu.VMEM((DIM, LANES), F32),
            pltpu.VMEM((OWNERS, 16 * PAIRS, LANES), BF16),
            pltpu.VMEM((OWNERS, 16 * PAIRS, LANES), BF16),
            pltpu.VMEM((OWNERS, 16, LANES), BF16),
            pltpu.VMEM((OWNERS, 16, LANES), BF16),
            pltpu.VMEM((OWNERS, 16, LANES), F32),
            pltpu.VMEM((2 * HELD, LANES), F32),
            pltpu.VMEM((CODES, HELD), I32),
            pltpu.VMEM((HELD, LISTS_HERE), BF16),
            pltpu.VMEM((DIM, HELD), F32),
            pltpu.VMEM((CHUNKS, CHUNK_ROWS, CODES), F32),
            pltpu.VMEM((PLANE, CHUNK_ROWS, CODES), F32),
            pltpu.VMEM((PLANE, CHUNK_ROWS, CODES), F32),
            pltpu.VMEM((PLANE, CHUNK_ROWS, CODES), F32),
            pltpu.VMEM((6, 16, LANES), F32),
            pltpu.VMEM((PLANE, 16, LANES), F32),
            pltpu.VMEM((GROUPS, 1, LANES), F32),
            pltpu.VMEM((GROUPS, 1, LANES), F32),
            pltpu.VMEM((CHUNKS, 8, CODES), F32),
            pltpu.VMEM((PLANE, 8, CODES), F32),
            pltpu.VMEM((PLANE, 8, CODES), F32),
            pltpu.VMEM((PLANE, 8, CODES), F32),
            pltpu.VMEM((2, 8, LANES), F32),
            pltpu.VMEM((PLANE, 8, LANES), F32),
            dma((5,)),
            dma, dma, dma, dma,
            dma((3,)), dma((3,)), dma((4,)), dma((4,)),
            dma((PLANE,)), dma((PLANE,)),
            dma, dma,
            dma((6,)), dma,
            dma, dma((6,)),
            dma, dma((PLANE,)), dma, dma((PLANE,)), dma, dma,
            dma, dma, dma, dma, dma((6,)), dma,
        ],
        compiler_params=pltpu.CompilerParams(collective_id=0, has_side_effects=True, vmem_limit_bytes=VMEM_LIMIT),
    )(list_ids.reshape(1, ROWS), vectors, codes, centroids,
      codebook0.reshape(CHUNKS, CHUNK_SUBS * WIDTH, CODES))
    return book.reshape(SUBS, WIDTH, CODES), list_error.reshape(ROWS)


def solution(mesh):
    in_specs = (
        P(("groups", "owners"), None),
        P(("groups", "owners")),
        P(None, ("groups", "owners")),
        P(("groups", "owners"), None),
        P(),
    )
    out_specs = (P(), P(("groups", "owners")))
    return jax.shard_map(local, mesh=mesh, in_specs=in_specs, out_specs=out_specs, check_vma=False)
```

```python
import jax
import jax.numpy as jnp
from jax import lax
from jax.experimental import pallas as pl
from jax.experimental.pallas import tpu as pltpu
from jax.sharding import PartitionSpec as P

MESH = pl.DeviceIdType.MESH
F32 = jnp.float32
BF16 = jnp.bfloat16
I32 = jnp.int32

ROWS = 128
DIM = 768
SUBS = 96
WIDTH = 8
CODES = 256
OWNERS = 64
GROUPS = 8
CAP = 6
SLOTS = 8
LANES = 128
PAIRS = 2
LISTS_HERE = GROUPS * ROWS
CHUNKS = 32
CHUNK_SUBS = SUBS // CHUNKS
CHUNK_ROWS = 2 * CHUNK_SUBS * WIDTH
PLANE = 16
PRIOR = 128.0
UNIT_PLACES = (0, 2, 5, 8, 10, 13)
VEC_FIRST = 7
HELD = CAP * OWNERS
VMEM_LIMIT = 48 * 1024 * 1024


def vmem():
    return pl.BlockSpec(memory_space=pltpu.VMEM)


def wait_bytes(ref, sem):
    pltpu.make_async_copy(ref, ref, sem).wait()


def place():
    group, owner = lax.axis_index("groups"), lax.axis_index("owners")
    return group, owner


def local_copy(src, dst, sem):
    copy = pltpu.make_async_copy(src, dst, sem)
    copy.start()
    return copy


def each(first, last, body):
    def step(k, carry):
        body(k)
        return carry
    lax.fori_loop(first, last, step, 0)


def index_kernel(ids_hbm, vec_hbm, codes_hbm, cent_hbm, book0_hbm, book_ref, out_ref,
                 ids_v, vec_v, codes_v, book0_v, table, place_v, spare_v, vec_t, vec_out, vec_mid, vec_in, code_out, code_in,
                 code_f, spare_f, held_codes, pick_v, base_t, sums, half, plane, plane_in, line, line_in, parts, parts_in,
                 tally, tally_half, tally_plane, tally_plane_in, tally_line, tally_line_in,
                 load_sem, code_send, code_recv, row_send, row_recv, vec_send, vec_recv, x_send, x_recv, sib_send, sib_recv,
                 core_send, core_recv, plane_send, plane_recv, line_send, line_recv,
                 unit_send, unit_recv, gather_send, gather_recv, back_send, back_recv, part_send, part_recv,
                 t_core_send, t_core_recv, t_plane_send, t_plane_recv, t_line_send, t_line_recv):
    group, owner = place()
    x, core = group // 2, group % 2
    y, z = owner // 16, owner % 16
    xy = x * 4 + y
    sibling = group + 1 - 2 * core
    chunk = core * PLANE + xy

    def plane_device(i):
        return ((i // 4) * 2 + core, (i % 4) * 16 + z)

    def plane_to(k):
        step = (7 * k) % PLANE
        return (x + step // 4) % 4 * 4 + (y + step % 4) % 4

    def plane_from(k):
        step = (7 * k) % PLANE
        return (x + 4 - step // 4) % 4 * 4 + (y + 4 - step % 4) % 4

    def far_first(j):
        return (8 + (1 - 2 * (j % 2)) * ((j + 1) // 2)) % 16

    load_ids = local_copy(ids_hbm, ids_v, load_sem.at[0])
    load_codes = local_copy(codes_hbm, codes_v, load_sem.at[1])
    load_vec = local_copy(vec_hbm, vec_v, load_sem.at[2])
    load_cent = local_copy(cent_hbm, table.at[group], load_sem.at[3])
    load_book = local_copy(book0_hbm.at[chunk], book0_v, load_sem.at[4])

    barrier = pltpu.get_barrier_semaphore()

    def nth_peer(k):
        return (y + 3 - k % 4) % 4 * 16 + (z + far_first(k // 4)) % 16

    each(0, OWNERS - 1, lambda k: pl.semaphore_signal(
        barrier, inc=1, device_id=(group, nth_peer(k)), device_id_type=MESH))
    for k in range(1, GROUPS):
        pl.semaphore_signal(barrier, inc=1, device_id=((group + k) % GROUPS, owner), device_id_type=MESH)
    for i in range(1, 4):
        for j in range(1, 4):
            pl.semaphore_signal(
                barrier, inc=1, device_id=((group + 2 * i) % GROUPS, (owner + 16 * j) % OWNERS), device_id_type=MESH)

    load_ids.wait()
    ids = ids_v[...]
    owner_of = (ids >> 7) & (OWNERS - 1)
    in_owner = (lax.broadcasted_iota(I32, (OWNERS, LANES), 0) == owner_of).astype(F32)
    before = (lax.broadcasted_iota(I32, (LANES, LANES), 0) < lax.broadcasted_iota(I32, (LANES, LANES), 1))
    running = jnp.dot(in_owner.astype(BF16), before.astype(F32).astype(BF16), preferred_element_type=F32)
    rank = jnp.sum(in_owner * running, axis=0, keepdims=True).astype(I32)
    slot = owner_of * SLOTS + rank
    place_v[...] = (lax.broadcasted_iota(I32, (OWNERS * SLOTS, LANES), 0) == slot).astype(F32).astype(BF16)
    for q in range(3):
        here = jnp.where((rank >> 1) == q, slot + 6 - 2 * q, -1)
        spare_v[q] = (lax.broadcasted_iota(I32, (OWNERS * SLOTS, LANES), 0) == here).astype(F32).astype(BF16)
    list_no = ((ids >> 13) << 7) + (ids & 127) + 1

    def extra(part):
        block = 4 + part // 3
        return jnp.dot(spare_v[part % 3], vec_v[:, 128 * block: 128 * block + 128], preferred_element_type=F32)

    def pack(one, two):
        return jnp.concatenate([one.reshape(OWNERS, SLOTS, LANES), two.reshape(OWNERS, SLOTS, LANES)],
                               axis=1).astype(BF16)

    load_codes.wait()
    load_vec.wait()
    row8 = lax.broadcasted_iota(I32, (8, LANES), 0)
    list_rows = jnp.where(row8 == 0, list_no >> 8, jnp.where(row8 == 1, list_no & 255, 0)).astype(F32)
    load = jnp.concatenate(
        [codes_v[...].astype(F32), list_rows, jnp.zeros((CODES - 2 * SUBS - 8, LANES), F32)], axis=0).astype(BF16)
    rows = lax.dot_general(place_v[...], load, (((1,), (1,)), ((), ())), preferred_element_type=F32)
    code_out[...] = pack(rows[:, 0:128] + extra(0), rows[:, 128:256] + extra(1))

    load_cent.wait()
    pl.semaphore_wait(barrier, OWNERS - 1 + GROUPS - 1 + 9)

    def code_copy(k):
        peer = nth_peer(k)
        return pltpu.make_async_remote_copy(
            code_out.at[peer], code_in.at[owner], code_send, code_recv, device_id=(group, peer), device_id_type=MESH)

    def row_copy(j):
        to = (y + j) % 4
        return pltpu.make_async_remote_copy(
            vec_out.at[to], vec_mid.at[y], row_send, row_recv, device_id=(group, to * 16 + z), device_id_type=MESH)

    def vec_copy(k):
        to = (z + far_first(k)) % 16
        return pltpu.make_async_remote_copy(
            vec_mid.at[:, to], vec_in.at[:, z], vec_send, vec_recv, device_id=(group, y * 16 + to), device_id_type=MESH)

    across = []
    for j in range(1, 4):
        across.append(pltpu.make_async_remote_copy(
            table.at[group], table.at[group], x_send.at[j - 1], x_recv.at[j - 1],
            device_id=((group + 2 * j) % GROUPS, owner), device_id_type=MESH))
    aside = [pltpu.make_async_remote_copy(
        table.at[group], table.at[group], sib_send.at[0], sib_recv.at[0],
        device_id=(sibling, owner), device_id_type=MESH)]
    each(0, OWNERS - 1, lambda k: code_copy(k).start())
    for copy in across + aside:
        copy.start()
    code_in[owner] = code_out[owner]

    for p in range(PAIRS):
        rows = jnp.dot(place_v[...], vec_v[:, 256 * p: 256 * p + 256], preferred_element_type=F32)
        vec_out[:, :, 16 * p: 16 * p + 16, :] = pack(
            rows[:, 0:128] + extra(2 + 2 * p), rows[:, 128:256] + extra(3 + 2 * p)).reshape(4, 16, 16, LANES)
    for j in (2, 1, 3):
        row_copy(j).start()
    vec_mid[y] = vec_out[y]
    left_half = lax.broadcasted_iota(I32, (WIDTH, LANES), 1) < 64

    def by_code(pairs):
        lefts, rights = [], []
        low_level = lax.broadcasted_iota(I32, (64, pairs[0][1].shape[1]), 0)
        for rows, code in pairs:
            high = code >> 6
            lefts += [jnp.where(high == h, rows, 0.0) for h in range(4)]
            rights.append((low_level == (code & 63)).astype(F32))
        out = lax.dot_general(
            jnp.concatenate(lefts, axis=0).astype(BF16), jnp.concatenate(rights, axis=0).astype(BF16),
            (((1,), (1,)), ((), ())), preferred_element_type=F32)
        results = []
        for q in range(4):
            column = 128 * (q // 2)
            tiles = []
            for t in range(2):
                one = out[32 * q + 16 * t: 32 * q + 16 * t + 8, column: column + 128]
                two = out[32 * q + 16 * t + 8: 32 * q + 16 * t + 16, column: column + 128]
                if q % 2 == 0:
                    two = pltpu.roll(two, 64, 1)
                else:
                    one = pltpu.roll(one, 64, 1)
                tiles.append(jnp.where(left_half, one, two))
            results.append(jnp.concatenate(tiles, axis=1))
        return results

    def pairs_of(chunks):
        return [(ch, mm, r) for ch in chunks for mm in range(CHUNK_SUBS) for r in range(2)]

    ones = jnp.ones((WIDTH, LANES), F32)
    tile_row = lax.broadcasted_iota(I32, (8, CODES), 0)

    def count(c):
        pairs = pairs_of([2 * c, 2 * c + 1])
        tiles = [jnp.zeros((8, CODES), F32)] * 2
        for first in range(0, len(pairs), 4):
            four = pairs[first: first + 4]
            got = by_code([(ones, codes_v[pl.ds(r * SUBS + ch * CHUNK_SUBS + mm, 1), :]) for ch, mm, r in four])
            for n, (ch, mm, r) in enumerate(four):
                at = (first + n) // 6
                tiles[at] = jnp.where(tile_row == r * CHUNK_SUBS + mm, got[n], tiles[at])
        tally[2 * c] = tiles[0]
        tally[2 * c + 1] = tiles[1]

    each(0, CHUNKS // 2, count)

    t_core = pltpu.make_async_remote_copy(
        tally.at[pl.ds((1 - core) * PLANE, PLANE)], tally_half, t_core_send, t_core_recv,
        device_id=(sibling, owner), device_id_type=MESH)
    t_core.start()
    for j in range(6):
        vec_t[128 * j: 128 * j + 128, :] = vec_v[:, 128 * j: 128 * j + 128].astype(F32).T

    def t_plane_copy(k):
        i = plane_to(k)
        return pltpu.make_async_remote_copy(
            tally_plane.at[i], tally_plane_in.at[xy], t_plane_send, t_plane_recv,
            device_id=plane_device(i), device_id_type=MESH)

    def t_line_copy(unit):
        return pltpu.make_async_remote_copy(
            tally_line.at[unit % 2], tally_line_in.at[z], t_line_send.at[unit], t_line_recv,
            device_id=(group, y * 16 + UNIT_PLACES[unit]), device_id_type=MESH)

    def vector_sums(c):
        pairs = pairs_of([2 * c, 2 * c + 1])
        for first in range(0, len(pairs), 4):
            four = pairs[first: first + 4]
            got = by_code([(vec_t[pl.ds(8 * (ch * CHUNK_SUBS + mm), 8), :],
                            codes_v[pl.ds(r * SUBS + ch * CHUNK_SUBS + mm, 1), :]) for ch, mm, r in four])
            for n, (ch, mm, r) in enumerate(four):
                sums[ch, 16 * mm + 8 * r: 16 * mm + 8 * r + 8, :] = got[n]

    def total_of(ref):
        total = ref[0]
        for i in range(1, PLANE):
            total = total + ref[i]
        return total

    each(0, CHUNKS // 4, vector_sums)
    t_core.wait_recv()
    tally_plane[...] = tally[pl.ds(core * PLANE, PLANE)] + tally_half[...]
    each(1, PLANE, lambda k: t_plane_copy(k).start())
    tally_plane_in[xy] = tally_plane[xy]
    for j in range(1, 4):
        source = (group + 2 * GROUPS - 2 * j) % GROUPS
        across[j - 1].wait_recv()
        relay = pltpu.make_async_remote_copy(
            table.at[source], table.at[source], sib_send.at[j], sib_recv.at[j],
            device_id=(sibling, owner), device_id_type=MESH)
        relay.start()
        aside.append(relay)
    each(CHUNKS // 4, CHUNKS // 2, vector_sums)
    wait_bytes(tally_plane.at[pl.ds(0, PLANE - 1)], t_plane_recv)
    total = total_of(tally_plane_in)
    tally_line[0] = total[:, 0:128]
    tally_line[1] = total[:, 128:256]
    for unit, where in enumerate(UNIT_PLACES):
        @pl.when(z != where)
        def _(unit=unit):
            t_line_copy(unit).start()
    wait_bytes(vec_mid.at[pl.ds(0, 3)], row_recv)
    each(0, VEC_FIRST, lambda k: vec_copy(k).start())
    vec_in[:, pl.ds(z, 1)] = vec_mid[:, pl.ds(z, 1)]

    wait_bytes(code_in.at[pl.ds(0, OWNERS - 1)], code_recv)

    code_f[...] = code_in[...].astype(F32)
    for h in range(2):
        rows = jnp.concatenate([code_f[:, 8 * h + s, :] for s in range(CAP)], axis=0)
        held_codes[128 * h: 128 * h + 128, :] = rows.T.astype(I32)
        if h == 1:
            which = rows[:, 64:65] * 256.0 + rows[:, 65:66]
    lane = lax.broadcasted_iota(I32, (HELD, LISTS_HERE), 1).astype(F32) + 1.0
    pick_v[...] = (which == lane).astype(F32).astype(BF16)
    for copy in aside:
        copy.wait_recv()
    rows = jnp.dot(pick_v[...], table[...].reshape(LISTS_HERE, DIM), preferred_element_type=F32)
    for j in range(6):
        base_t[128 * j: 128 * j + 128, :] = rows[:, 128 * j: 128 * j + 128].T

    def centroid_sums(chunks):
        pairs = pairs_of(chunks)
        for first in range(0, len(pairs), 4):
            four = pairs[first: first + 4]
            got = by_code([(base_t[pl.ds(8 * (ch * CHUNK_SUBS + mm), 8), :],
                            held_codes[pl.ds(r * SUBS + ch * CHUNK_SUBS + mm, 1), :]) for ch, mm, r in four])
            for n, (ch, mm, r) in enumerate(four):
                sums[ch, 16 * mm + 8 * r: 16 * mm + 8 * r + 8, :] -= got[n]

    def core_copy(k):
        i = plane_to(k + 1)
        return pltpu.make_async_remote_copy(
            sums.at[(1 - core) * PLANE + i], half.at[i], core_send.at[k], core_recv.at[k],
            device_id=(sibling, owner), device_id_type=MESH)

    def plane_copy(k):
        i = plane_to(k + 1)
        return pltpu.make_async_remote_copy(
            plane.at[i], plane_in.at[xy], plane_send, plane_recv, device_id=plane_device(i), device_id_type=MESH)

    def other_half(c):
        k = 2 * c
        centroid_sums([(1 - core) * PLANE + plane_to(k + 1), (1 - core) * PLANE + plane_to(k + 2)])
        core_copy(k).start()
        core_copy(k + 1).start()

    def own_half(c):
        k = 2 * c
        centroid_sums([core * PLANE + plane_to(k + 1), core * PLANE + plane_to(k + 2)])
        for n in (k, k + 1):
            i = plane_to(n + 1)
            core_copy(n).wait_recv()
            plane[i] = sums[core * PLANE + i] + half[i]

            @pl.when(n < PLANE - 1)
            def _(n=n):
                plane_copy(n).start()

    def both_halves(c):
        @pl.when(c < PLANE // 2)
        def _():
            other_half(c)

        @pl.when(c > 0)
        def _():
            own_half(c - 1)

    each(0, PLANE // 2 + 1, both_halves)
    plane_in[xy] = plane[xy]
    wait_bytes(plane.at[pl.ds(0, PLANE - 1)], plane_recv)
    total = total_of(plane_in)
    for unit in range(6):
        mm, side = unit // 2, unit % 2
        line[unit] = total[16 * mm: 16 * mm + 16, 128 * side: 128 * side + 128]

    def line_copy(unit):
        return pltpu.make_async_remote_copy(
            line.at[unit], line_in.at[z], line_send.at[unit], line_recv,
            device_id=(group, y * 16 + UNIT_PLACES[unit]), device_id_type=MESH)

    for unit, where in enumerate(UNIT_PLACES):
        @pl.when(z != where)
        def _(unit=unit):
            line_copy(unit).start()

    each(VEC_FIRST, PLANE - 1, lambda k: vec_copy(k).start())

    def unit_ref(unit):
        mm, side = unit // 2, unit % 2
        return book_ref.at[chunk, 8 * mm: 8 * mm + 8, 128 * side: 128 * side + 128]

    def unit_copy(unit, k):
        return pltpu.make_async_remote_copy(
            unit_ref(unit), unit_ref(unit), unit_send, unit_recv.at[unit],
            device_id=(group, y * 16 + (z + far_first(k)) % 16), device_id_type=MESH)

    load_book.wait()
    for unit, where in enumerate(UNIT_PLACES):
        mm, side = unit // 2, unit % 2

        @pl.when(z == where)
        def _(unit=unit, mm=mm, side=side, where=where):
            line_in[where] = line[unit]
            tally_line_in[where] = tally_line[side]
            wait_bytes(tally_line_in.at[pl.ds(0, PLANE - 1)], t_line_recv)
            counts = total_of(tally_line_in)
            wait_bytes(line_in.at[pl.ds(0, PLANE - 1)], line_recv)
            total = total_of(line_in)
            here = slice(128 * side, 128 * side + 128)
            start = book0_v[8 * mm: 8 * mm + 8, here]
            first = (total[0:8] + PRIOR * start) / (counts[mm: mm + 1] + PRIOR)
            book_ref[chunk, 8 * mm: 8 * mm + 8, here] = (
                (total[8:16] + PRIOR * first) / (counts[3 + mm: 4 + mm] + PRIOR))
            each(0, PLANE - 1, lambda k: unit_copy(unit, k).start())

    for unit, where in enumerate(UNIT_PLACES):
        @pl.when(z != where)
        def _(unit=unit):
            wait_bytes(unit_ref(unit), unit_recv.at[unit])

    def gather_copy(k):
        return pltpu.make_async_remote_copy(
            book_ref.at[chunk], book_ref.at[chunk], gather_send, gather_recv.at[k],
            device_id=plane_device(plane_to(k)), device_id_type=MESH)

    def back_copy(k):
        part = book_ref.at[core * PLANE + plane_from(k)]
        return pltpu.make_async_remote_copy(
            part, part, back_send, back_recv.at[k], device_id=(sibling, owner), device_id_type=MESH)

    each(1, PLANE, lambda k: gather_copy(k).start())
    back_copy(0).start()

    def take_spare(part):
        for h in range(2):
            for i in range(2):
                t = 2 * (part + h) + i
                spare_f[OWNERS * t: OWNERS * t + OWNERS, :] = code_f[:, 8 * h + 6 + i, :]

    code_f[...] = code_in[...].astype(F32)
    take_spare(0)
    wait_bytes(vec_in.at[:, pl.ds(0, PLANE - 1)], vec_recv)
    for p in range(PAIRS):
        code_f[...] = vec_in[:, :, 16 * p: 16 * p + 16, :].reshape(OWNERS, 16, LANES).astype(F32)
        take_spare(2 + 2 * p)
        for h in range(2):
            j = 2 * p + h
            rows = jnp.concatenate([code_f[:, 8 * h + s, :] for s in range(CAP)], axis=0)
            base_t[128 * j: 128 * j + 128, :] = rows.T - base_t[128 * j: 128 * j + 128, :]
    for j in range(4, 6):
        rows = spare_f[HELD * (j - 4): HELD * (j - 4) + HELD, :]
        base_t[128 * j: 128 * j + 128, :] = rows.T - base_t[128 * j: 128 * j + 128, :]

    def add(ch, totals):
        for mm in range(CHUNK_SUBS):
            m = ch * CHUNK_SUBS + mm
            left = book_ref[ch, 8 * mm: 8 * mm + 8, 0:128]
            right = book_ref[ch, 8 * mm: 8 * mm + 8, 128:256]
            row = jnp.broadcast_to(held_codes[pl.ds(SUBS + m, 1), :], (WIDTH, HELD))
            rest = base_t[pl.ds(8 * m, 8), :]
            new = []
            for t in range(HELD // LANES):
                code = row[:, 128 * t: 128 * t + 128]
                low = code & 127
                one = jnp.take_along_axis(left, low, axis=1)
                two = jnp.take_along_axis(right, low, axis=1)
                diff = rest[:, 128 * t: 128 * t + 128] - jnp.where(code > 127, two, one)
                new.append(totals[t] + diff * diff)
            totals = tuple(new)
        return totals

    def arrivals(k, totals):
        i = plane_from(k)
        part = book_ref.at[core * PLANE + i]
        wait_bytes(part, gather_recv.at[k])
        back_copy(k).start()
        before_it = (1 - core) * PLANE + plane_from(k - 1)
        wait_bytes(part, back_recv.at[k - 1])
        return add(before_it, add(core * PLANE + i, totals))

    zero = jnp.zeros((WIDTH, LANES), F32)
    totals = add(chunk, (zero,) * 3)
    totals = lax.fori_loop(1, PLANE, arrivals, totals)
    wait_bytes(book_ref.at[0], back_recv.at[PLANE - 1])
    totals = add((1 - core) * PLANE + plane_from(PLANE - 1), totals)
    error = jnp.concatenate([jnp.sum(t, axis=0, keepdims=True) for t in totals], axis=1) / float(DIM)
    top = error.astype(BF16).astype(F32)
    mid = (error - top).astype(BF16).astype(F32)
    low = error - top - mid
    row = lax.broadcasted_iota(I32, (16, HELD), 0)
    split = jnp.where(row == 0, top, jnp.where(row == 1, mid, jnp.where(row == 2, low, 0.0))).astype(BF16)
    by_list = jnp.sum(jnp.dot(split, pick_v[...], preferred_element_type=F32), axis=0, keepdims=True)
    for i in range(GROUPS):
        parts[i] = by_list[:, 128 * i: 128 * i + 128]

    def part_copy(k):
        return pltpu.make_async_remote_copy(
            parts.at[(group + k) % GROUPS], parts_in.at[group], part_send, part_recv,
            device_id=((group + k) % GROUPS, owner), device_id_type=MESH)

    for k in range(1, GROUPS):
        part_copy(k).start()
    parts_in[group] = parts[group]

    t_core.wait_send()
    wait_bytes(tally_plane.at[pl.ds(0, PLANE - 1)], t_plane_send)
    wait_bytes(code_in.at[pl.ds(0, OWNERS - 1)], code_send)
    wait_bytes(vec_mid.at[pl.ds(0, 3)], row_send)
    wait_bytes(vec_in.at[:, pl.ds(0, PLANE - 1)], vec_send)
    for copy in across + aside:
        copy.wait_send()
    each(0, PLANE, lambda k: core_copy(k).wait_send())
    wait_bytes(plane.at[pl.ds(0, PLANE - 1)], plane_send)
    for unit, where in enumerate(UNIT_PLACES):
        @pl.when(z != where)
        def _(unit=unit):
            line_copy(unit).wait_send()
            t_line_copy(unit).wait_send()

        @pl.when(z == where)
        def _(unit=unit):
            each(0, PLANE - 1, lambda k: unit_copy(unit, k).wait_send())
    wait_bytes(book_ref.at[pl.ds(0, PLANE - 1)], gather_send)
    wait_bytes(book_ref.at[pl.ds(0, PLANE)], back_send)

    wait_bytes(parts.at[pl.ds(0, GROUPS - 1)], part_recv)
    sum_here = parts_in[0]
    for i in range(1, GROUPS):
        sum_here = sum_here + parts_in[i]
    out_ref[...] = sum_here
    wait_bytes(parts.at[pl.ds(0, GROUPS - 1)], part_send)


def local(vectors, list_ids, codes, centroids, codebook0):
    dma = pltpu.SemaphoreType.DMA
    any_place = pl.BlockSpec(memory_space=pltpu.HBM)
    book, list_error = pl.pallas_call(
        index_kernel,
        out_shape=(jax.ShapeDtypeStruct((CHUNKS, CHUNK_SUBS * WIDTH, CODES), F32),
                   jax.ShapeDtypeStruct((1, LANES), F32)),
        in_specs=[any_place] * 5,
        out_specs=(vmem(), vmem()),
        scratch_shapes=[
            pltpu.VMEM((1, LANES), I32),
            pltpu.VMEM((ROWS, DIM), BF16),
            pltpu.VMEM((2 * SUBS, LANES), I32),
            pltpu.VMEM((CHUNK_SUBS * WIDTH, CODES), F32),
            pltpu.VMEM((GROUPS, ROWS, DIM), BF16),
            pltpu.VMEM((OWNERS * SLOTS, LANES), BF16),
            pltpu.VMEM((3, OWNERS * SLOTS, LANES), BF16),
            pltpu.VMEM((DIM, LANES), F32),
            pltpu.VMEM((4, 16, 16 * PAIRS, LANES), BF16),
            pltpu.VMEM((4, 16, 16 * PAIRS, LANES), BF16),
            pltpu.VMEM((4, 16, 16 * PAIRS, LANES), BF16),
            pltpu.VMEM((OWNERS, 16, LANES), BF16),
            pltpu.VMEM((OWNERS, 16, LANES), BF16),
            pltpu.VMEM((OWNERS, 16, LANES), F32),
            pltpu.VMEM((2 * HELD, LANES), F32),
            pltpu.VMEM((CODES, HELD), I32),
            pltpu.VMEM((HELD, LISTS_HERE), BF16),
            pltpu.VMEM((DIM, HELD), F32),
            pltpu.VMEM((CHUNKS, CHUNK_ROWS, CODES), F32),
            pltpu.VMEM((PLANE, CHUNK_ROWS, CODES), F32),
            pltpu.VMEM((PLANE, CHUNK_ROWS, CODES), F32),
            pltpu.VMEM((PLANE, CHUNK_ROWS, CODES), F32),
            pltpu.VMEM((6, 16, LANES), F32),
            pltpu.VMEM((PLANE, 16, LANES), F32),
            pltpu.VMEM((GROUPS, 1, LANES), F32),
            pltpu.VMEM((GROUPS, 1, LANES), F32),
            pltpu.VMEM((CHUNKS, 8, CODES), F32),
            pltpu.VMEM((PLANE, 8, CODES), F32),
            pltpu.VMEM((PLANE, 8, CODES), F32),
            pltpu.VMEM((PLANE, 8, CODES), F32),
            pltpu.VMEM((2, 8, LANES), F32),
            pltpu.VMEM((PLANE, 8, LANES), F32),
            dma((5,)),
            dma, dma, dma, dma, dma, dma,
            dma((3,)), dma((3,)), dma((4,)), dma((4,)),
            dma((PLANE,)), dma((PLANE,)),
            dma, dma,
            dma((6,)), dma,
            dma, dma((6,)),
            dma, dma((PLANE,)), dma, dma((PLANE,)), dma, dma,
            dma, dma, dma, dma, dma((6,)), dma,
        ],
        compiler_params=pltpu.CompilerParams(collective_id=0, has_side_effects=True, vmem_limit_bytes=VMEM_LIMIT),
    )(*[pltpu.with_memory_space_constraint(ref, pltpu.HBM) for ref in (
        list_ids.reshape(1, ROWS), vectors, codes, centroids,
        codebook0.reshape(CHUNKS, CHUNK_SUBS * WIDTH, CODES))])
    return book.reshape(SUBS, WIDTH, CODES), list_error.reshape(ROWS)


def solution(mesh):
    in_specs = (
        P(("groups", "owners"), None),
        P(("groups", "owners")),
        P(None, ("groups", "owners")),
        P(("groups", "owners"), None),
        P(),
    )
    out_specs = (P(), P(("groups", "owners")))
    return jax.shard_map(local, mesh=mesh, in_specs=in_specs, out_specs=out_specs, check_vma=False)
```

```python
import jax
import jax.numpy as jnp
from jax import lax
from jax.experimental import pallas as pl
from jax.experimental.pallas import tpu as pltpu
from jax.sharding import PartitionSpec as P

MESH = pl.DeviceIdType.MESH
F32 = jnp.float32
BF16 = jnp.bfloat16
I32 = jnp.int32

ROWS = 128
DIM = 768
SUBS = 96
WIDTH = 8
CODES = 256
OWNERS = 64
GROUPS = 8
CAP = 6
SLOTS = 8
LANES = 128
PAIRS = 2
LISTS_HERE = GROUPS * ROWS
CHUNKS = 32
CHUNK_SUBS = SUBS // CHUNKS
CHUNK_ROWS = 2 * CHUNK_SUBS * WIDTH
PLANE = 16
PRIOR = 128.0
UNIT_PLACES = (0, 2, 5, 8, 10, 13)
VEC_FIRST = 7
HELD = CAP * OWNERS
VMEM_LIMIT = 48 * 1024 * 1024


def vmem():
    return pl.BlockSpec(memory_space=pltpu.VMEM)


def wait_bytes(ref, sem):
    pltpu.make_async_copy(ref, ref, sem).wait()


def place():
    group, owner = lax.axis_index("groups"), lax.axis_index("owners")
    return group, owner


def local_copy(src, dst, sem):
    copy = pltpu.make_async_copy(src, dst, sem)
    copy.start()
    return copy


def each(first, last, body):
    def step(k, carry):
        body(k)
        return carry
    lax.fori_loop(first, last, step, 0)


def index_kernel(ids_hbm, vec_hbm, codes_hbm, cent_hbm, book0_hbm, book_ref, out_ref,
                 ids_v, vec_v, codes_v, book0_v, table, place_v, spare_v, vec_t, vec_out, vec_mid, vec_in, code_out, code_in,
                 code_f, spare_f, held_codes, pick_v, base_t, sums, half, plane, plane_in, line, line_in, parts, parts_in,
                 tally, tally_half, tally_plane, tally_plane_in, tally_line, tally_line_in,
                 load_sem, code_send, code_recv, row_send, row_recv, vec_send, vec_recv, x_send, x_recv, sib_send, sib_recv,
                 core_send, core_recv, plane_send, plane_recv, line_send, line_recv,
                 unit_send, unit_recv, gather_send, gather_recv, back_send, back_recv, part_send, part_recv,
                 t_core_send, t_core_recv, t_plane_send, t_plane_recv, t_line_send, t_line_recv):
    group, owner = place()
    x, core = group // 2, group % 2
    y, z = owner // 16, owner % 16
    xy = x * 4 + y
    sibling = group + 1 - 2 * core
    chunk = core * PLANE + xy

    def plane_device(i):
        return (lax.div(i, 4) * 2 + core, lax.rem(i, 4) * 16 + z)

    def plane_to(k):
        step = lax.rem(7 * k, PLANE)
        return lax.rem(x + lax.div(step, 4), 4) * 4 + lax.rem(y + lax.rem(step, 4), 4)

    def plane_from(k):
        step = lax.rem(7 * k, PLANE)
        return lax.rem(x + 4 - lax.div(step, 4), 4) * 4 + lax.rem(y + 4 - lax.rem(step, 4), 4)

    def far_first(j):
        return lax.rem(8 + (1 - 2 * lax.rem(j, 2)) * lax.div(j + 1, 2), 16)

    load_ids = local_copy(ids_hbm, ids_v, load_sem.at[0])
    load_codes = local_copy(codes_hbm, codes_v, load_sem.at[1])
    load_vec = local_copy(vec_hbm, vec_v, load_sem.at[2])
    load_cent = local_copy(cent_hbm, table.at[group], load_sem.at[3])
    load_book = local_copy(book0_hbm.at[chunk], book0_v, load_sem.at[4])

    barrier = pltpu.get_barrier_semaphore()

    def nth_peer(k):
        return lax.rem(y + 3 - lax.rem(k, 4), 4) * 16 + lax.rem(z + far_first(lax.div(k, 4)), 16)

    each(0, OWNERS - 1, lambda k: pl.semaphore_signal(
        barrier, inc=1, device_id=(group, nth_peer(k)), device_id_type=MESH))
    for k in range(1, GROUPS):
        pl.semaphore_signal(barrier, inc=1, device_id=((group + k) % GROUPS, owner), device_id_type=MESH)
    for i in range(1, 4):
        for j in range(1, 4):
            pl.semaphore_signal(
                barrier, inc=1, device_id=((group + 2 * i) % GROUPS, (owner + 16 * j) % OWNERS), device_id_type=MESH)

    load_ids.wait()
    ids = ids_v[...]
    owner_of = (ids >> 7) & (OWNERS - 1)
    in_owner = (lax.broadcasted_iota(I32, (OWNERS, LANES), 0) == owner_of).astype(F32)
    before = (lax.broadcasted_iota(I32, (LANES, LANES), 0) < lax.broadcasted_iota(I32, (LANES, LANES), 1))
    running = jnp.dot(in_owner.astype(BF16), before.astype(F32).astype(BF16), preferred_element_type=F32)
    rank = jnp.sum(in_owner * running, axis=0, keepdims=True).astype(I32)
    slot = owner_of * SLOTS + rank
    place_v[...] = (lax.broadcasted_iota(I32, (OWNERS * SLOTS, LANES), 0) == slot).astype(F32).astype(BF16)
    for q in range(3):
        here = jnp.where((rank >> 1) == q, slot + 6 - 2 * q, -1)
        spare_v[q] = (lax.broadcasted_iota(I32, (OWNERS * SLOTS, LANES), 0) == here).astype(F32).astype(BF16)
    list_no = ((ids >> 13) << 7) + (ids & 127) + 1

    def extra(part):
        block = 4 + part // 3
        return jnp.dot(spare_v[part % 3], vec_v[:, 128 * block: 128 * block + 128], preferred_element_type=F32)

    def pack(one, two):
        return jnp.concatenate([one.reshape(OWNERS, SLOTS, LANES), two.reshape(OWNERS, SLOTS, LANES)],
                               axis=1).astype(BF16)

    load_codes.wait()
    load_vec.wait()
    row8 = lax.broadcasted_iota(I32, (8, LANES), 0)
    list_rows = jnp.where(row8 == 0, list_no >> 8, jnp.where(row8 == 1, list_no & 255, 0)).astype(F32)
    load = jnp.concatenate(
        [codes_v[...].astype(F32), list_rows, jnp.zeros((CODES - 2 * SUBS - 8, LANES), F32)], axis=0).astype(BF16)
    rows = lax.dot_general(place_v[...], load, (((1,), (1,)), ((), ())), preferred_element_type=F32)
    code_out[...] = pack(rows[:, 0:128] + extra(0), rows[:, 128:256] + extra(1))

    load_cent.wait()
    pl.semaphore_wait(barrier, OWNERS - 1 + GROUPS - 1 + 9)

    def code_copy(k):
        peer = nth_peer(k)
        return pltpu.make_async_remote_copy(
            code_out.at[peer], code_in.at[owner], code_send, code_recv, device_id=(group, peer), device_id_type=MESH)

    def row_copy(j):
        to = (y + j) % 4
        return pltpu.make_async_remote_copy(
            vec_out.at[to], vec_mid.at[y], row_send, row_recv, device_id=(group, to * 16 + z), device_id_type=MESH)

    def vec_copy(k):
        to = lax.rem(z + far_first(k), 16)
        return pltpu.make_async_remote_copy(
            vec_mid.at[:, to], vec_in.at[:, z], vec_send, vec_recv, device_id=(group, y * 16 + to), device_id_type=MESH)

    across = []
    for j in range(1, 4):
        across.append(pltpu.make_async_remote_copy(
            table.at[group], table.at[group], x_send.at[j - 1], x_recv.at[j - 1],
            device_id=((group + 2 * j) % GROUPS, owner), device_id_type=MESH))
    aside = [pltpu.make_async_remote_copy(
        table.at[group], table.at[group], sib_send.at[0], sib_recv.at[0],
        device_id=(sibling, owner), device_id_type=MESH)]
    each(0, OWNERS - 1, lambda k: code_copy(k).start())
    for copy in across + aside:
        copy.start()
    code_in[owner] = code_out[owner]

    for p in range(PAIRS):
        rows = jnp.dot(place_v[...], vec_v[:, 256 * p: 256 * p + 256], preferred_element_type=F32)
        vec_out[:, :, 16 * p: 16 * p + 16, :] = pack(
            rows[:, 0:128] + extra(2 + 2 * p), rows[:, 128:256] + extra(3 + 2 * p)).reshape(4, 16, 16, LANES)
    for j in (2, 1, 3):
        row_copy(j).start()
    vec_mid[y] = vec_out[y]
    left_half = lax.broadcasted_iota(I32, (WIDTH, LANES), 1) < 64

    def by_code(pairs):
        lefts, rights = [], []
        low_level = lax.broadcasted_iota(I32, (64, pairs[0][1].shape[1]), 0)
        for rows, code in pairs:
            high = code >> 6
            lefts += [jnp.where(high == h, rows, 0.0) for h in range(4)]
            rights.append((low_level == (code & 63)).astype(F32))
        out = lax.dot_general(
            jnp.concatenate(lefts, axis=0).astype(BF16), jnp.concatenate(rights, axis=0).astype(BF16),
            (((1,), (1,)), ((), ())), preferred_element_type=F32)
        results = []
        for q in range(4):
            column = 128 * (q // 2)
            tiles = []
            for t in range(2):
                one = out[32 * q + 16 * t: 32 * q + 16 * t + 8, column: column + 128]
                two = out[32 * q + 16 * t + 8: 32 * q + 16 * t + 16, column: column + 128]
                if q % 2 == 0:
                    two = pltpu.roll(two, 64, 1)
                else:
                    one = pltpu.roll(one, 64, 1)
                tiles.append(jnp.where(left_half, one, two))
            results.append(jnp.concatenate(tiles, axis=1))
        return results

    def pairs_of(chunks):
        return [(ch, mm, r) for ch in chunks for mm in range(CHUNK_SUBS) for r in range(2)]

    ones = jnp.ones((WIDTH, LANES), F32)
    tile_row = lax.broadcasted_iota(I32, (8, CODES), 0)

    def count(c):
        pairs = pairs_of([2 * c, 2 * c + 1])
        tiles = [jnp.zeros((8, CODES), F32)] * 2
        for first in range(0, len(pairs), 4):
            four = pairs[first: first + 4]
            got = by_code([(ones, codes_v[pl.ds(r * SUBS + ch * CHUNK_SUBS + mm, 1), :]) for ch, mm, r in four])
            for n, (ch, mm, r) in enumerate(four):
                at = (first + n) // 6
                tiles[at] = jnp.where(tile_row == r * CHUNK_SUBS + mm, got[n], tiles[at])
        tally[2 * c] = tiles[0]
        tally[2 * c + 1] = tiles[1]

    each(0, CHUNKS // 2, count)

    t_core = pltpu.make_async_remote_copy(
        tally.at[pl.ds((1 - core) * PLANE, PLANE)], tally_half, t_core_send, t_core_recv,
        device_id=(sibling, owner), device_id_type=MESH)
    t_core.start()
    for j in range(6):
        vec_t[128 * j: 128 * j + 128, :] = vec_v[:, 128 * j: 128 * j + 128].astype(F32).T

    def t_plane_copy(k):
        i = plane_to(k)
        return pltpu.make_async_remote_copy(
            tally_plane.at[i], tally_plane_in.at[xy], t_plane_send, t_plane_recv,
            device_id=plane_device(i), device_id_type=MESH)

    def t_line_copy(unit):
        return pltpu.make_async_remote_copy(
            tally_line.at[unit % 2], tally_line_in.at[z], t_line_send.at[unit], t_line_recv,
            device_id=(group, y * 16 + UNIT_PLACES[unit]), device_id_type=MESH)

    def vector_sums(c):
        pairs = pairs_of([2 * c, 2 * c + 1])
        for first in range(0, len(pairs), 4):
            four = pairs[first: first + 4]
            got = by_code([(vec_t[pl.ds(8 * (ch * CHUNK_SUBS + mm), 8), :],
                            codes_v[pl.ds(r * SUBS + ch * CHUNK_SUBS + mm, 1), :]) for ch, mm, r in four])
            for n, (ch, mm, r) in enumerate(four):
                sums[ch, 16 * mm + 8 * r: 16 * mm + 8 * r + 8, :] = got[n]

    def total_of(ref):
        total = ref[0]
        for i in range(1, PLANE):
            total = total + ref[i]
        return total

    each(0, CHUNKS // 4, vector_sums)
    t_core.wait_recv()
    tally_plane[...] = tally[pl.ds(core * PLANE, PLANE)] + tally_half[...]
    each(1, PLANE, lambda k: t_plane_copy(k).start())
    tally_plane_in[xy] = tally_plane[xy]
    for j in range(1, 4):
        source = (group + 2 * GROUPS - 2 * j) % GROUPS
        across[j - 1].wait_recv()
        relay = pltpu.make_async_remote_copy(
            table.at[source], table.at[source], sib_send.at[j], sib_recv.at[j],
            device_id=(sibling, owner), device_id_type=MESH)
        relay.start()
        aside.append(relay)
    each(CHUNKS // 4, CHUNKS // 2, vector_sums)
    wait_bytes(tally_plane.at[pl.ds(0, PLANE - 1)], t_plane_recv)
    total = total_of(tally_plane_in)
    tally_line[0] = total[:, 0:128]
    tally_line[1] = total[:, 128:256]
    for unit, where in enumerate(UNIT_PLACES):
        @pl.when(z != where)
        def _(unit=unit):
            t_line_copy(unit).start()
    wait_bytes(vec_mid.at[pl.ds(0, 3)], row_recv)
    each(0, VEC_FIRST, lambda k: vec_copy(k).start())
    vec_in[:, pl.ds(z, 1)] = vec_mid[:, pl.ds(z, 1)]

    wait_bytes(code_in.at[pl.ds(0, OWNERS - 1)], code_recv)

    code_f[...] = code_in[...].astype(F32)
    for h in range(2):
        rows = jnp.concatenate([code_f[:, 8 * h + s, :] for s in range(CAP)], axis=0)
        held_codes[128 * h: 128 * h + 128, :] = rows.T.astype(I32)
        if h == 1:
            which = rows[:, 64:65] * 256.0 + rows[:, 65:66]
    lane = lax.broadcasted_iota(I32, (HELD, LISTS_HERE), 1).astype(F32) + 1.0
    pick_v[...] = (which == lane).astype(F32).astype(BF16)
    for copy in aside:
        copy.wait_recv()
    rows = jnp.dot(pick_v[...], table[...].reshape(LISTS_HERE, DIM), preferred_element_type=F32)
    for j in range(6):
        base_t[128 * j: 128 * j + 128, :] = rows[:, 128 * j: 128 * j + 128].T

    def centroid_sums(chunks):
        pairs = pairs_of(chunks)
        for first in range(0, len(pairs), 4):
            four = pairs[first: first + 4]
            got = by_code([(base_t[pl.ds(8 * (ch * CHUNK_SUBS + mm), 8), :],
                            held_codes[pl.ds(r * SUBS + ch * CHUNK_SUBS + mm, 1), :]) for ch, mm, r in four])
            for n, (ch, mm, r) in enumerate(four):
                sums[ch, 16 * mm + 8 * r: 16 * mm + 8 * r + 8, :] -= got[n]

    def core_copy(k):
        i = plane_to(k + 1)
        return pltpu.make_async_remote_copy(
            sums.at[(1 - core) * PLANE + i], half.at[i], core_send.at[k], core_recv.at[k],
            device_id=(sibling, owner), device_id_type=MESH)

    def plane_copy(k):
        i = plane_to(k + 1)
        return pltpu.make_async_remote_copy(
            plane.at[i], plane_in.at[xy], plane_send, plane_recv, device_id=plane_device(i), device_id_type=MESH)

    def other_half(c):
        k = 2 * c
        centroid_sums([(1 - core) * PLANE + plane_to(k + 1), (1 - core) * PLANE + plane_to(k + 2)])
        core_copy(k).start()
        core_copy(k + 1).start()

    def own_half(c):
        k = 2 * c
        centroid_sums([core * PLANE + plane_to(k + 1), core * PLANE + plane_to(k + 2)])
        for n in (k, k + 1):
            i = plane_to(n + 1)
            core_copy(n).wait_recv()
            plane[i] = sums[core * PLANE + i] + half[i]

            @pl.when(n < PLANE - 1)
            def _(n=n):
                plane_copy(n).start()

    def both_halves(c):
        @pl.when(c < PLANE // 2)
        def _():
            other_half(c)

        @pl.when(c > 0)
        def _():
            own_half(c - 1)

    each(0, PLANE // 2 + 1, both_halves)
    plane_in[xy] = plane[xy]
    wait_bytes(plane.at[pl.ds(0, PLANE - 1)], plane_recv)
    total = total_of(plane_in)
    for unit in range(6):
        mm, side = unit // 2, unit % 2
        line[unit] = total[16 * mm: 16 * mm + 16, 128 * side: 128 * side + 128]

    def line_copy(unit):
        return pltpu.make_async_remote_copy(
            line.at[unit], line_in.at[z], line_send.at[unit], line_recv,
            device_id=(group, y * 16 + UNIT_PLACES[unit]), device_id_type=MESH)

    for unit, where in enumerate(UNIT_PLACES):
        @pl.when(z != where)
        def _(unit=unit):
            line_copy(unit).start()

    each(VEC_FIRST, PLANE - 1, lambda k: vec_copy(k).start())

    def unit_ref(unit):
        mm, side = unit // 2, unit % 2
        return book_ref.at[chunk, 8 * mm: 8 * mm + 8, 128 * side: 128 * side + 128]

    def unit_copy(unit, k):
        return pltpu.make_async_remote_copy(
            unit_ref(unit), unit_ref(unit), unit_send, unit_recv.at[unit],
            device_id=(group, y * 16 + (z + far_first(k)) % 16), device_id_type=MESH)

    load_book.wait()
    for unit, where in enumerate(UNIT_PLACES):
        mm, side = unit // 2, unit % 2

        @pl.when(z == where)
        def _(unit=unit, mm=mm, side=side, where=where):
            line_in[where] = line[unit]
            tally_line_in[where] = tally_line[side]
            wait_bytes(tally_line_in.at[pl.ds(0, PLANE - 1)], t_line_recv)
            counts = total_of(tally_line_in)
            wait_bytes(line_in.at[pl.ds(0, PLANE - 1)], line_recv)
            total = total_of(line_in)
            here = slice(128 * side, 128 * side + 128)
            start = book0_v[8 * mm: 8 * mm + 8, here]
            first = (total[0:8] + PRIOR * start) / (counts[mm: mm + 1] + PRIOR)
            book_ref[chunk, 8 * mm: 8 * mm + 8, here] = (
                (total[8:16] + PRIOR * first) / (counts[3 + mm: 4 + mm] + PRIOR))
            each(0, PLANE - 1, lambda k: unit_copy(unit, k).start())

    for unit, where in enumerate(UNIT_PLACES):
        @pl.when(z != where)
        def _(unit=unit):
            wait_bytes(unit_ref(unit), unit_recv.at[unit])

    def gather_copy(k):
        return pltpu.make_async_remote_copy(
            book_ref.at[chunk], book_ref.at[chunk], gather_send, gather_recv.at[k],
            device_id=plane_device(plane_to(k)), device_id_type=MESH)

    def back_copy(k):
        part = book_ref.at[core * PLANE + plane_from(k)]
        return pltpu.make_async_remote_copy(
            part, part, back_send, back_recv.at[k], device_id=(sibling, owner), device_id_type=MESH)

    each(1, PLANE, lambda k: gather_copy(k).start())
    back_copy(0).start()

    def take_spare(part):
        for h in range(2):
            for i in range(2):
                t = 2 * (part + h) + i
                spare_f[OWNERS * t: OWNERS * t + OWNERS, :] = code_f[:, 8 * h + 6 + i, :]

    code_f[...] = code_in[...].astype(F32)
    take_spare(0)
    wait_bytes(vec_in.at[:, pl.ds(0, PLANE - 1)], vec_recv)
    for p in range(PAIRS):
        code_f[...] = vec_in[:, :, 16 * p: 16 * p + 16, :].reshape(OWNERS, 16, LANES).astype(F32)
        take_spare(2 + 2 * p)
        for h in range(2):
            j = 2 * p + h
            rows = jnp.concatenate([code_f[:, 8 * h + s, :] for s in range(CAP)], axis=0)
            base_t[128 * j: 128 * j + 128, :] = rows.T - base_t[128 * j: 128 * j + 128, :]
    for j in range(4, 6):
        rows = spare_f[HELD * (j - 4): HELD * (j - 4) + HELD, :]
        base_t[128 * j: 128 * j + 128, :] = rows.T - base_t[128 * j: 128 * j + 128, :]

    def add(ch, totals):
        for mm in range(CHUNK_SUBS):
            m = ch * CHUNK_SUBS + mm
            left = book_ref[ch, 8 * mm: 8 * mm + 8, 0:128]
            right = book_ref[ch, 8 * mm: 8 * mm + 8, 128:256]
            row = jnp.broadcast_to(held_codes[pl.ds(SUBS + m, 1), :], (WIDTH, HELD))
            rest = base_t[pl.ds(8 * m, 8), :]
            new = []
            for t in range(HELD // LANES):
                code = row[:, 128 * t: 128 * t + 128]
                low = code & 127
                one = jnp.take_along_axis(left, low, axis=1)
                two = jnp.take_along_axis(right, low, axis=1)
                diff = rest[:, 128 * t: 128 * t + 128] - jnp.where(code > 127, two, one)
                new.append(totals[t] + diff * diff)
            totals = tuple(new)
        return totals

    def arrivals(k, totals):
        i = plane_from(k)
        part = book_ref.at[core * PLANE + i]
        wait_bytes(part, gather_recv.at[k])
        back_copy(k).start()
        before_it = (1 - core) * PLANE + plane_from(k - 1)
        wait_bytes(part, back_recv.at[k - 1])
        return add(before_it, add(core * PLANE + i, totals))

    zero = jnp.zeros((WIDTH, LANES), F32)
    totals = add(chunk, (zero,) * 3)
    totals = lax.fori_loop(1, PLANE, arrivals, totals)
    wait_bytes(book_ref.at[0], back_recv.at[PLANE - 1])
    totals = add((1 - core) * PLANE + plane_from(PLANE - 1), totals)
    error = jnp.concatenate([jnp.sum(t, axis=0, keepdims=True) for t in totals], axis=1) / float(DIM)
    top = error.astype(BF16).astype(F32)
    mid = (error - top).astype(BF16).astype(F32)
    low = error - top - mid
    row = lax.broadcasted_iota(I32, (16, HELD), 0)
    split = jnp.where(row == 0, top, jnp.where(row == 1, mid, jnp.where(row == 2, low, 0.0))).astype(BF16)
    by_list = jnp.sum(jnp.dot(split, pick_v[...], preferred_element_type=F32), axis=0, keepdims=True)
    for i in range(GROUPS):
        parts[i] = by_list[:, 128 * i: 128 * i + 128]

    def part_copy(k):
        return pltpu.make_async_remote_copy(
            parts.at[(group + k) % GROUPS], parts_in.at[group], part_send, part_recv,
            device_id=((group + k) % GROUPS, owner), device_id_type=MESH)

    for k in range(1, GROUPS):
        part_copy(k).start()
    parts_in[group] = parts[group]

    t_core.wait_send()
    wait_bytes(tally_plane.at[pl.ds(0, PLANE - 1)], t_plane_send)
    wait_bytes(code_in.at[pl.ds(0, OWNERS - 1)], code_send)
    wait_bytes(vec_mid.at[pl.ds(0, 3)], row_send)
    wait_bytes(vec_in.at[:, pl.ds(0, PLANE - 1)], vec_send)
    for copy in across + aside:
        copy.wait_send()
    each(0, PLANE, lambda k: core_copy(k).wait_send())
    wait_bytes(plane.at[pl.ds(0, PLANE - 1)], plane_send)
    for unit, where in enumerate(UNIT_PLACES):
        @pl.when(z != where)
        def _(unit=unit):
            line_copy(unit).wait_send()
            t_line_copy(unit).wait_send()

        @pl.when(z == where)
        def _(unit=unit):
            each(0, PLANE - 1, lambda k: unit_copy(unit, k).wait_send())
    wait_bytes(book_ref.at[pl.ds(0, PLANE - 1)], gather_send)
    wait_bytes(book_ref.at[pl.ds(0, PLANE)], back_send)

    wait_bytes(parts.at[pl.ds(0, GROUPS - 1)], part_recv)
    sum_here = parts_in[0]
    for i in range(1, GROUPS):
        sum_here = sum_here + parts_in[i]
    out_ref[...] = sum_here
    wait_bytes(parts.at[pl.ds(0, GROUPS - 1)], part_send)


def local(vectors, list_ids, codes, centroids, codebook0):
    dma = pltpu.SemaphoreType.DMA
    any_place = pl.BlockSpec(memory_space=pltpu.HBM)
    book, list_error = pl.pallas_call(
        index_kernel,
        out_shape=(jax.ShapeDtypeStruct((CHUNKS, CHUNK_SUBS * WIDTH, CODES), F32),
                   jax.ShapeDtypeStruct((1, LANES), F32)),
        in_specs=[any_place] * 5,
        out_specs=(vmem(), vmem()),
        scratch_shapes=[
            pltpu.VMEM((1, LANES), I32),
            pltpu.VMEM((ROWS, DIM), BF16),
            pltpu.VMEM((2 * SUBS, LANES), I32),
            pltpu.VMEM((CHUNK_SUBS * WIDTH, CODES), F32),
            pltpu.VMEM((GROUPS, ROWS, DIM), BF16),
            pltpu.VMEM((OWNERS * SLOTS, LANES), BF16),
            pltpu.VMEM((3, OWNERS * SLOTS, LANES), BF16),
            pltpu.VMEM((DIM, LANES), F32),
            pltpu.VMEM((4, 16, 16 * PAIRS, LANES), BF16),
            pltpu.VMEM((4, 16, 16 * PAIRS, LANES), BF16),
            pltpu.VMEM((4, 16, 16 * PAIRS, LANES), BF16),
            pltpu.VMEM((OWNERS, 16, LANES), BF16),
            pltpu.VMEM((OWNERS, 16, LANES), BF16),
            pltpu.VMEM((OWNERS, 16, LANES), F32),
            pltpu.VMEM((2 * HELD, LANES), F32),
            pltpu.VMEM((CODES, HELD), I32),
            pltpu.VMEM((HELD, LISTS_HERE), BF16),
            pltpu.VMEM((DIM, HELD), F32),
            pltpu.VMEM((CHUNKS, CHUNK_ROWS, CODES), F32),
            pltpu.VMEM((PLANE, CHUNK_ROWS, CODES), F32),
            pltpu.VMEM((PLANE, CHUNK_ROWS, CODES), F32),
            pltpu.VMEM((PLANE, CHUNK_ROWS, CODES), F32),
            pltpu.VMEM((6, 16, LANES), F32),
            pltpu.VMEM((PLANE, 16, LANES), F32),
            pltpu.VMEM((GROUPS, 1, LANES), F32),
            pltpu.VMEM((GROUPS, 1, LANES), F32),
            pltpu.VMEM((CHUNKS, 8, CODES), F32),
            pltpu.VMEM((PLANE, 8, CODES), F32),
            pltpu.VMEM((PLANE, 8, CODES), F32),
            pltpu.VMEM((PLANE, 8, CODES), F32),
            pltpu.VMEM((2, 8, LANES), F32),
            pltpu.VMEM((PLANE, 8, LANES), F32),
            dma((5,)),
            dma, dma, dma, dma, dma, dma,
            dma((3,)), dma((3,)), dma((4,)), dma((4,)),
            dma((PLANE,)), dma((PLANE,)),
            dma, dma,
            dma((6,)), dma,
            dma, dma((6,)),
            dma, dma((PLANE,)), dma, dma((PLANE,)), dma, dma,
            dma, dma, dma, dma, dma((6,)), dma,
        ],
        compiler_params=pltpu.CompilerParams(collective_id=0, has_side_effects=True, vmem_limit_bytes=VMEM_LIMIT),
    )(*[pltpu.with_memory_space_constraint(ref, pltpu.HBM) for ref in (
        list_ids.reshape(1, ROWS), vectors, codes, centroids,
        codebook0.reshape(CHUNKS, CHUNK_SUBS * WIDTH, CODES))])
    return book.reshape(SUBS, WIDTH, CODES), list_error.reshape(ROWS)


def solution(mesh):
    in_specs = (
        P(("groups", "owners"), None),
        P(("groups", "owners")),
        P(None, ("groups", "owners")),
        P(("groups", "owners"), None),
        P(),
    )
    out_specs = (P(), P(("groups", "owners")))
    return jax.shard_map(local, mesh=mesh, in_specs=in_specs, out_specs=out_specs, check_vma=False)
```
